32 devices in a mesh: dp: 4 (over x, core), seq: 8 (over z, y).
Axes of the slice: x: 2, y: 2, z: 4, core: 2. Of those that a mesh axis runs over, the one named last changes fastest.
Arguments:
- queries: bfloat16 [4, 2048, 1024], P('dp', 'seq'), may hold values from -6 to 6
- keys: bfloat16 [4, 2048, 1024], P('dp', 'seq'), may hold values from -6 to 6
- values: bfloat16 [4, 2048, 1024], P('dp', 'seq'), may hold values from -6 to 6
- out_weight: bfloat16 [1024, 1024], replicated, may hold values from -0.1875 to 0.1875
- cotangent: bfloat16 [4, 2048, 1024], P('dp', 'seq'), may hold values from -6 to 6
Outputs:
- mixed: bfloat16 [4, 2048, 1024], P('dp', 'seq')
- grad_out_weight: float32 [1024, 1024], P(('dp', 'seq'))
- grad_queries: bfloat16 [4, 2048, 1024], P('dp', 'seq')
- grad_keys: bfloat16 [4, 2048, 1024], P('dp', 'seq')
- grad_values: bfloat16 [4, 2048, 1024], P('dp', 'seq')
The draws below stay inside these ranges and needn't reach their ends.
All inputs are finite; a program needn't handle non-finite values.
Results may differ from the reference program's by a relative error of at most 0.02.
Values may be sent and summed in bfloat16 or wider, within the bound.
A program may use at most 128 MiB of HBM per device.

```python
import math
import jax
import jax.numpy as jnp
from jax import lax

WIDTH = 1024
HEADS = 16
HEAD_DIM = 64
BLOCK = 64
TOK_DEV = 256
BATCH = 4
SEQ = 2048
GROUP_ONE = 2
GROUP_TWO = 4


def draw_queries(key, part):
    own_key = jax.random.fold_in(key, 11)
    noise = jax.random.normal(own_key, (BATCH, SEQ, HEADS * HEAD_DIM), jnp.float32)
    field = jnp.clip(1.25 * noise, -5.5, 5.5)
    return field.astype(jnp.bfloat16)


def draw_keys(key, part):
    own_key = jax.random.fold_in(key, 21)
    noise = jax.random.normal(own_key, (BATCH, SEQ, HEADS * HEAD_DIM), jnp.float32)
    field = jnp.clip(1.25 * noise, -5.5, 5.5)
    return field.astype(jnp.bfloat16)


def level_of(key, shape, pieces, smallest, top_value):
    def one(position, blocks):
        steps = jax.random.uniform(jax.random.fold_in(jax.random.fold_in(key, 6), position), (blocks,), jnp.float32, smallest / len(pieces), top_value / len(pieces))
        return jnp.repeat(jnp.exp(steps), shape[position] // blocks).reshape((-1,) + (1,) * (len(shape) - position - 1))

    factor_of = one(*pieces[0])
    for cut in pieces[1:]:
        factor_of = factor_of * one(*cut)
    return factor_of


def scatter_about(stream_key, dims, scale, bound, cuts=(), held_as=jnp.bfloat16):
    gain = level_of(stream_key, dims, cuts, -0.22, 0.18) if cuts else 1.0
    entries = jax.random.normal(stream_key, dims, jnp.float32) * scale * gain
    return jnp.minimum(jnp.maximum(entries, -bound), bound).astype(held_as)


def setup_inputs(seed: int = 0) -> dict:
    streams_of = jax.random.split(jax.random.key(seed), 6)
    return {
        "queries": draw_queries(jax.random.fold_in(streams_of[5], 71), 0),
        "keys": draw_keys(jax.random.fold_in(streams_of[5], 71), 0),
        "values": scatter_about(streams_of[2], (BATCH, SEQ, HEADS * HEAD_DIM), 1.0, 6.0, ((0, 4), (1, 8))),
        "out_weight": scatter_about(streams_of[3], (HEADS * HEAD_DIM, WIDTH), (HEADS * HEAD_DIM) ** -0.5, 0.1875),
        "cotangent": scatter_about(streams_of[4], (BATCH, SEQ, WIDTH), 1.0, 6.0, ((0, 4), (1, 8))),
    }


MASKED = -1e+30

def rounded(matrix):
    return lax.optimization_barrier(matrix.astype(jnp.bfloat16)).astype(jnp.float32)

def split_heads(matrix, head_count):
    return matrix.reshape(matrix.shape[0], head_count, matrix.shape[1] // head_count)

def pool_rows(matrix, pool_width):
    coarse_count = matrix.shape[0] // pool_width
    summed = lax.optimization_barrier(jnp.sum(matrix.reshape(coarse_count, pool_width, matrix.shape[1]), axis=1, dtype=jnp.float32))
    return (summed / math.sqrt(pool_width)).astype(jnp.bfloat16)

def stretch(matrix, pool_width):
    widened = jnp.broadcast_to(matrix[:, None], (matrix.shape[0], pool_width) + matrix.shape[1:])
    return widened.reshape((matrix.shape[0] * pool_width,) + matrix.shape[1:])

def key_usable(first_block, block_count, all_blocks, block_len, left_open, right_open):
    block_ids = first_block + jnp.arange(block_count)[:, None]
    slot_ids = jnp.arange(3 * block_len)[None, :] // block_len
    keep_left = jnp.logical_or(slot_ids > 0, jnp.logical_or(block_ids > 0, left_open))
    keep_right = jnp.logical_or(slot_ids < 2, jnp.logical_or(block_ids < all_blocks - 1, right_open))
    return jnp.logical_and(keep_left, keep_right)

def windows(extended, row_count, block_len, head_count):
    block_count = row_count // block_len
    head_size = extended.shape[1] // head_count
    slabs = [extended[shift_id * block_len:shift_id * block_len + row_count].reshape(block_count, block_len, head_count, head_size) for shift_id in range(3)]
    return jnp.concatenate(slabs, axis=1)

def unfold(window_grads, row_count, block_len):
    folded = jnp.zeros((row_count + 2 * block_len, window_grads.shape[2] * window_grads.shape[3]), jnp.float32)
    for shift_id in range(3):
        slab = window_grads[:, shift_id * block_len:(shift_id + 1) * block_len].reshape(row_count, -1)
        folded = folded + jnp.pad(slab, ((shift_id * block_len, (2 - shift_id) * block_len), (0, 0)))
    return folded

def to_rows(blocked):
    return jnp.transpose(blocked, (0, 2, 1)).reshape(-1, blocked.shape[1])

def to_blocks(per_row, block_len):
    return jnp.transpose(per_row.reshape(-1, block_len, per_row.shape[1]), (0, 2, 1))

def allowed_mask(level_id, query_ids, key_ids, per_device, span_one, span_two):
    query_dev = query_ids[:, None] // per_device
    key_dev = key_ids[None, :] // per_device
    if level_id == 0:
        return jnp.logical_and(query_dev // span_one == key_dev // span_one, jnp.abs(query_ids[:, None] - key_ids[None, :]) > 1)
    if level_id == 1:
        return jnp.logical_and(query_dev // span_two == key_dev // span_two, query_dev // span_one != key_dev // span_one)
    return query_dev // span_two != key_dev // span_two

def combine(fine_max, fine_total, fine_weighted, levels):
    row_max = fine_max
    for level_max, level_total, level_weighted, pool_width in levels:
        row_max = jnp.maximum(row_max, stretch(level_max, pool_width))
    factor = jnp.exp(fine_max - row_max)
    denominator = fine_total * factor
    numerator = fine_weighted * factor[..., None]
    for level_max, level_total, level_weighted, pool_width in levels:
        factor = jnp.exp(stretch(level_max, pool_width) - row_max)
        denominator = denominator + stretch(level_total, pool_width) * factor
        numerator = numerator + stretch(level_weighted, pool_width) * factor[..., None]
    attended = (numerator / denominator[..., None]).reshape(numerator.shape[0], -1).astype(jnp.bfloat16)
    return (attended, row_max, denominator)

def band_scores(queries, extended, usable, block_len, head_count, score_scale):
    row_count = queries.shape[0]
    key_value_win = windows(extended, row_count, block_len, 2 * head_count)
    key_win = key_value_win[:, :, :head_count]
    value_win = key_value_win[:, :, head_count:]
    query_blocks = queries.reshape(row_count // block_len, block_len, head_count, -1)
    scores = jnp.einsum('bqhe,bkhe->bhqk', query_blocks.astype(jnp.float32), key_win.astype(jnp.float32)) * score_scale
    scores = jnp.where(usable[:, None, None, :], scores, MASKED)
    return (scores, query_blocks, key_win, value_win)

def band_forward(queries, extended, usable, block_len, head_count, score_scale):
    scores, query_blocks, key_win, value_win = band_scores(queries, extended, usable, block_len, head_count, score_scale)
    maxima = lax.optimization_barrier(jnp.max(scores, axis=-1))
    exponent = jnp.exp(scores - maxima[..., None])
    totals = lax.optimization_barrier(jnp.sum(exponent, axis=-1))
    weighted = jnp.einsum('bhqk,bkhe->bqhe', rounded(exponent), value_win.astype(jnp.float32))
    return (to_rows(maxima), to_rows(totals), weighted.reshape(queries.shape[0], head_count, -1))

def band_backward(queries, extended, usable, upstream, row_delta, maxima, weight, block_len, head_count, score_scale):
    row_count = queries.shape[0]
    scores, query_blocks, key_win, value_win = band_scores(queries, extended, usable, block_len, head_count, score_scale)
    probability = jnp.exp(scores - to_blocks(maxima, block_len)[..., None]) * to_blocks(weight, block_len)[..., None]
    grad_blocks = upstream.reshape(row_count // block_len, block_len, head_count, -1).astype(jnp.float32)
    prob_grad = jnp.einsum('bqhe,bkhe->bhqk', grad_blocks, value_win.astype(jnp.float32))
    score_grad = rounded(probability * (prob_grad - to_blocks(row_delta, block_len)[..., None]))
    grad_query = jnp.einsum('bhqk,bkhe->bqhe', score_grad, key_win.astype(jnp.float32)) * score_scale
    grad_key = jnp.einsum('bhqk,bqhe->bkhe', score_grad, query_blocks.astype(jnp.float32)) * score_scale
    grad_value = jnp.einsum('bhqk,bqhe->bkhe', rounded(probability), grad_blocks)
    joined = jnp.concatenate([grad_key, grad_value], axis=2)
    return (grad_query.reshape(row_count, -1), unfold(joined, row_count, block_len))

def coarse_scores(coarse_query, coarse_key, allowed, head_count, score_scale):
    scores = jnp.einsum('qhe,khe->hqk', split_heads(coarse_query, head_count).astype(jnp.float32), split_heads(coarse_key, head_count).astype(jnp.float32)) * score_scale
    scores = jnp.where(allowed[None], scores, MASKED)
    maxima = lax.optimization_barrier(jnp.max(scores, axis=-1))
    exponent = jnp.where(allowed[None], jnp.exp(scores - maxima[..., None]), 0.0)
    return (maxima, exponent)

def coarse_forward(coarse_query, coarse_key, coarse_value, allowed, head_count, score_scale):
    maxima, exponent = coarse_scores(coarse_query, coarse_key, allowed, head_count, score_scale)
    weighted = jnp.einsum('hqk,khe->qhe', rounded(exponent), split_heads(coarse_value, head_count).astype(jnp.float32))
    return (maxima.T, lax.optimization_barrier(jnp.sum(exponent, axis=-1)).T, weighted)

def coarse_backward(coarse_query, coarse_key, coarse_value, allowed, head_count, score_scale, weight, upstream, row_delta, pool_width):
    maxima, exponent = coarse_scores(coarse_query, coarse_key, allowed, head_count, score_scale)
    coarse_count = coarse_query.shape[0]
    gathered = rounded(lax.optimization_barrier(jnp.sum((weight[..., None] * upstream).reshape(coarse_count, pool_width, head_count, -1), axis=1)))
    delta_sum = lax.optimization_barrier(jnp.sum((weight * row_delta).reshape(coarse_count, pool_width, head_count), axis=1))
    prob_grad = jnp.einsum('qhe,khe->hqk', gathered, split_heads(coarse_value, head_count).astype(jnp.float32))
    score_grad = rounded(exponent * (prob_grad - delta_sum.T[..., None]))
    grad_query = jnp.einsum('hqk,khe->qhe', score_grad, split_heads(coarse_key, head_count).astype(jnp.float32)) * score_scale
    grad_key = jnp.einsum('hqk,qhe->khe', score_grad, split_heads(coarse_query, head_count).astype(jnp.float32)) * score_scale
    grad_value = jnp.einsum('hqk,qhe->khe', rounded(exponent), gathered)
    key_count = coarse_key.shape[0]
    return (grad_query.reshape(coarse_count, -1), jnp.concatenate([grad_key.reshape(key_count, -1), grad_value.reshape(key_count, -1)], axis=1))

def one_performance(query_rows, key_rows, value_rows, grad_rows, out_weight):
    head_count = HEADS
    block_len = BLOCK
    hidden = HEADS * HEAD_DIM
    score_scale = 1.0 / math.sqrt(HEAD_DIM)
    segments = SEQ // TOK_DEV
    block_count = TOK_DEV // block_len
    widths = (block_len, 2 * block_len, 4 * block_len)
    joined = jnp.concatenate([key_rows, value_rows], axis=1)
    padded = jnp.pad(joined, ((block_len, block_len), (0, 0)))

    def segment_rows(matrix, segment):
        return lax.dynamic_slice_in_dim(matrix, segment * TOK_DEV, TOK_DEV, 0)

    def segment_inputs(segment):
        extended = lax.dynamic_slice_in_dim(padded, segment * TOK_DEV, TOK_DEV + 2 * block_len, 0)
        usable = key_usable(0, block_count, block_count, block_len, segment > 0, segment < segments - 1)
        return (segment_rows(query_rows, segment), extended, usable)

    def fine_forward(segment):
        rows_here, extended, usable = segment_inputs(segment)
        return band_forward(rows_here, extended, usable, block_len, head_count, score_scale)
    segment_ids = jnp.arange(segments, dtype=jnp.int32)
    fine_max, fine_total, fine_weighted = lax.map(fine_forward, segment_ids)
    fine_max = fine_max.reshape(SEQ, head_count)
    fine_total = fine_total.reshape(SEQ, head_count)
    fine_weighted = fine_weighted.reshape(SEQ, head_count, HEAD_DIM)
    coarse = []
    levels = []
    for level_id in range(3):
        pool_width = widths[level_id]
        coarse_query = pool_rows(query_rows, pool_width)
        coarse_kv = pool_rows(joined, pool_width)
        coarse_ids = jnp.arange(SEQ // pool_width)
        allowed = allowed_mask(level_id, coarse_ids, coarse_ids, TOK_DEV // pool_width, GROUP_ONE, GROUP_TWO)
        entry = (coarse_query, coarse_kv[:, :hidden], coarse_kv[:, hidden:], allowed)
        coarse.append(entry)
        levels.append(coarse_forward(entry[0], entry[1], entry[2], allowed, head_count, score_scale) + (pool_width,))
    attended, row_max, denominator = combine(fine_max, fine_total, fine_weighted, levels)
    mixed = jnp.dot(attended, out_weight, preferred_element_type=jnp.float32).astype(jnp.bfloat16)
    d_attended = lax.dot_general(grad_rows, out_weight, (((1,), (1,)), ((), ())), preferred_element_type=jnp.float32).astype(jnp.bfloat16)
    upstream = split_heads(d_attended, head_count).astype(jnp.float32)
    row_delta = lax.optimization_barrier(jnp.sum(upstream * split_heads(attended, head_count).astype(jnp.float32), axis=-1))
    fine_weight = jnp.exp(fine_max - row_max) / denominator

    def fine_backward(segment):
        rows_here, extended, usable = segment_inputs(segment)
        return band_backward(rows_here, extended, usable, segment_rows(d_attended, segment), segment_rows(row_delta, segment), segment_rows(fine_max, segment), segment_rows(fine_weight, segment), block_len, head_count, score_scale)
    grad_query, ext_grads = lax.map(fine_backward, segment_ids)
    middle = ext_grads[:, block_len:block_len + TOK_DEV]
    left_part = ext_grads[:, :block_len]
    right_part = ext_grads[:, TOK_DEV + block_len:]
    zero_part = jnp.zeros_like(left_part[:1])
    from_next = jnp.concatenate([left_part[1:], zero_part], axis=0)
    from_prev = jnp.concatenate([zero_part, right_part[:-1]], axis=0)
    middle = middle + jnp.pad(from_next, ((0, 0), (TOK_DEV - block_len, 0), (0, 0)))
    middle = middle + jnp.pad(from_prev, ((0, 0), (0, TOK_DEV - block_len), (0, 0)))
    kv_grad = middle.reshape(SEQ, 2 * hidden)
    query_grad = grad_query.reshape(SEQ, hidden)
    for entry, level in zip(coarse, levels):
        pool_width = level[3]
        weight = jnp.exp(stretch(level[0], pool_width) - row_max) / denominator
        coarse_q_grad, coarse_kv_grad = coarse_backward(entry[0], entry[1], entry[2], entry[3], head_count, score_scale, weight, upstream, row_delta, pool_width)
        query_grad = query_grad + stretch(coarse_q_grad, pool_width) / math.sqrt(pool_width)
        kv_grad = kv_grad + stretch(coarse_kv_grad, pool_width) / math.sqrt(pool_width)
    return (mixed, attended, query_grad.astype(jnp.bfloat16), kv_grad[:, :hidden].astype(jnp.bfloat16), kv_grad[:, hidden:].astype(jnp.bfloat16))

def reference(queries, keys, values, out_weight, cotangent):

    def run_one(inputs):
        return one_performance(inputs[0], inputs[1], inputs[2], inputs[3], out_weight)
    mixed, attended, grad_queries, grad_keys, grad_values = lax.map(run_one, (queries, keys, values, cotangent))
    hidden = HEADS * HEAD_DIM
    grad_out_weight = lax.dot_general(attended.reshape(-1, hidden), cotangent.reshape(-1, WIDTH), (((0,), (0,)), ((), ())), preferred_element_type=jnp.float32)
    return (mixed, grad_out_weight, grad_queries, grad_keys, grad_values)
```

```python
import functools
import math

import jax
import jax.numpy as jnp
from jax import lax
from jax.experimental import pallas as pl
from jax.experimental.pallas import tpu as pltpu
from jax.sharding import PartitionSpec as P

HEADS = 16
HEAD_DIM = 64
BLOCK = 64
MASKED = -1e30
SLOT = 16
F32 = jnp.float32
BF16 = jnp.bfloat16


def dot(a, b):
    return lax.dot_general(a, b, (((1,), (0,)), ((), ())), preferred_element_type=F32)


def dot_nt(a, b):
    return lax.dot_general(a, b, (((1,), (1,)), ((), ())), preferred_element_type=F32)


def dot_tn(a, b):
    return lax.dot_general(a, b, (((0,), (0,)), ((), ())), preferred_element_type=F32)


def iota(shape, dim):
    return lax.broadcasted_iota(jnp.int32, shape, dim)


def kernel(
    n, span_one, span_two,
    q_ref, k_ref, v_ref, w_ref, c_ref,
    mixed_ref, gw_ref, gq_ref, gk_ref, gv_ref,
    kext, vext, pool, da_ref, att_ref, bias, qx, ec, er, mcs, lcs, ncs, e_ref, inv_ref, wt_ref,
    g_ref, h_ref, gqa, dke, dve, hs, hr, dcs, dcr,
    pool_send, pool_recv, halo_send, halo_recv, back_send, back_recv, edge_send, edge_recv,
):
    rows, hidden = q_ref.shape
    blocks = rows // BLOCK
    pairs = hidden // 128
    halves = rows // 128
    widths = (BLOCK, 2 * BLOCK, 4 * BLOCK)
    scale = 1.0 / math.sqrt(HEAD_DIM)
    me = lax.axis_index("seq")
    heads = HEADS
    hr_rows = blocks * heads
    has_left, has_right = me > 0, me < n - 1

    barrier = pltpu.get_barrier_semaphore()
    for o in range(1, n):
        pl.semaphore_signal(
            barrier, inc=1, device_id={"seq": lax.rem(me + o, n)}, device_id_type=pl.DeviceIdType.MESH
        )
    pl.semaphore_wait(barrier, n - 1)

    def remote(src, dst, ssem, rsem, peer):
        return pltpu.make_async_remote_copy(
            src_ref=src, dst_ref=dst, send_sem=ssem, recv_sem=rsem,
            device_id={"seq": peer}, device_id_type=pl.DeviceIdType.MESH,
        )

    left = lax.rem(me + n - 1, n)
    right = lax.rem(me + 1, n)
    top = pl.ds(0, BLOCK)
    last = pl.ds(rows - BLOCK, BLOCK)
    bottom = pl.ds(rows + BLOCK, BLOCK)
    to_right = [
        remote(k_ref.at[last], kext.at[top], halo_send.at[0], halo_recv.at[0], right),
        remote(v_ref.at[last], vext.at[top], halo_send.at[1], halo_recv.at[1], right),
    ]
    to_left = [
        remote(k_ref.at[top], kext.at[bottom], halo_send.at[2], halo_recv.at[2], left),
        remote(v_ref.at[top], vext.at[bottom], halo_send.at[3], halo_recv.at[3], left),
    ]

    r_id, i_id = iota((SLOT, rows), 0), iota((SLOT, rows), 1)

    def pick(rid):
        base, hit = 0, jnp.zeros((SLOT, rows), jnp.bool_)
        for width in widths:
            count = rows // width
            inside = jnp.logical_and(rid >= base, rid < base + count)
            hit = jnp.logical_or(hit, jnp.logical_and(inside, i_id // width == rid - base))
            base += count
        return jnp.where(hit, 1.0, 0.0).astype(BF16)

    first1 = rows // widths[0]
    first2 = first1 + rows // widths[1]

    def row_scale(shape):
        rr = iota(shape, 0) % 8
        return jnp.where(
            rr < first1,
            1.0 / math.sqrt(widths[0]),
            jnp.where(rr < first2, 1.0 / math.sqrt(widths[1]), 1.0 / math.sqrt(widths[2])),
        )

    pooled = dot(pick(r_id), k_ref[...]) + dot(pick(r_id - 8), v_ref[...])
    pool[me] = (pooled * row_scale((SLOT, 1))).astype(BF16)

    for o in range(1, n):
        peer = lax.rem(me + o, n)
        remote(pool.at[me], pool.at[me], pool_send.at[o], pool_recv.at[o], peer).start()

    @pl.when(has_right)
    def _():
        for copy in to_right:
            copy.start()

    @pl.when(has_left)
    def _():
        for copy in to_left:
            copy.start()

    kext[BLOCK : BLOCK + rows] = k_ref[...]
    vext[BLOCK : BLOCK + rows] = v_ref[...]

    @pl.when(me == 0)
    def _():
        kext[0:BLOCK] = jnp.zeros((BLOCK, hidden), BF16)
        vext[0:BLOCK] = jnp.zeros((BLOCK, hidden), BF16)

    @pl.when(me == n - 1)
    def _():
        kext[rows + BLOCK :] = jnp.zeros((BLOCK, hidden), BF16)
        vext[rows + BLOCK :] = jnp.zeros((BLOCK, hidden), BF16)

    da_ref[...] = dot_nt(c_ref[...], w_ref[...]).astype(BF16)

    for b in range(halves):
        qb = (iota((256, 256), 0) % 128) // BLOCK + 1
        kb = iota((256, 256), 1) // BLOCK
        ok = jnp.abs(qb - kb) <= 1
        if b == 0:
            ok = jnp.logical_and(ok, jnp.logical_or(kb > 0, has_left))
        if b == halves - 1:
            ok = jnp.logical_and(ok, jnp.logical_or(kb < 3, has_right))
        bias[b] = jnp.where(ok, 0.0, MASKED)

    x_id, xi_id = iota((hr_rows, rows), 0) // heads, iota((hr_rows, rows), 1)
    head_mask = iota((hr_rows, hidden), 1) // HEAD_DIM == iota((hr_rows, hidden), 0) % heads
    for level, width in enumerate(widths):
        hit = xi_id // width == x_id * BLOCK // width
        rows_q = dot(jnp.where(hit, 1.0, 0.0).astype(BF16), q_ref[...]) * (1.0 / math.sqrt(width))
        rows_q = rows_q.astype(BF16).astype(F32) * scale
        qx[level] = jnp.where(head_mask, rows_q, 0.0).astype(BF16)

    cols = SLOT * n
    t_id = iota((hr_rows, cols), 0) // heads
    dev, rr = iota((hr_rows, cols), 1) // SLOT, iota((hr_rows, cols), 1) % SLOT
    same_one = dev // span_one == me // span_one
    same_two = dev // span_two == me // span_two
    gap = jnp.abs(me * first1 + t_id - dev * first1 - rr)
    allowed = (
        same_one & (rr < first1) & (gap > 1),
        same_two & jnp.logical_not(same_one) & (rr >= first1) & (rr < first2),
        jnp.logical_not(same_two) & (rr >= first2) & (rr < first2 + rows // widths[2]),
    )

    for o in range(1, n):
        src = lax.rem(me + n - o, n)
        remote(pool.at[src], pool.at[src], pool_send.at[o], pool_recv.at[o], src).wait_recv()
    coarse = pool[...].reshape(cols, hidden)
    s = jnp.full((hr_rows, cols), MASKED, F32)
    for level in range(3):
        s = jnp.where(allowed[level], dot_nt(qx[level], coarse), s)
    mc = jnp.max(s, axis=1, keepdims=True)
    ex = jnp.where(s > 0.5 * MASKED, jnp.exp(s - mc), 0.0)
    ec[...] = ex
    rolled = pltpu.roll(ex, 8, 1).astype(BF16)
    er[...] = rolled
    mcs[...] = jnp.broadcast_to(mc, (hr_rows, 128))
    lcs[...] = jnp.broadcast_to(jnp.sum(ex, axis=1, keepdims=True), (hr_rows, 128))

    def fold_heads(x):
        x = jnp.where(head_mask, x, 0.0)
        return [jnp.sum(x[t * heads : (t + 1) * heads], axis=0, keepdims=True) for t in range(blocks)]

    for t, row in enumerate(fold_heads(dot(rolled, coarse))):
        ncs[t : t + 1, :] = row

    @pl.when(has_left)
    def _():
        for copy in to_right:
            copy.wait_recv()

    @pl.when(has_right)
    def _():
        for copy in to_left:
            copy.wait_recv()

    low = iota((128, 128), 1) < HEAD_DIM

    def stack(x):
        zero = jnp.zeros_like(x)
        return jnp.concatenate([jnp.where(low, x, zero), jnp.where(low, zero, x)], axis=0)

    def choose(x):
        return jnp.where(low, x[:128], x[128:])

    def forward(p, carry):
        lanes = pl.ds(pl.multiple_of(p * 128, 128), 128)
        for b in range(halves):
            u = p * halves + b
            mine, win = pl.ds(128 * b, 128), pl.ds(128 * b, 256)
            q2 = stack(q_ref[mine, lanes] * scale)
            s = dot_nt(q2, kext[win, lanes]) + bias[b]

            def per_row(ref):
                parts = []
                for h in range(2):
                    for t in (2 * b, 2 * b + 1):
                        row = ref[pl.ds(t * heads + 2 * p + h, 1), :]
                        parts.append(jnp.broadcast_to(row, (BLOCK, 128)))
                return jnp.concatenate(parts, axis=0)

            mcr = per_row(mcs)
            m = jnp.maximum(jnp.max(s, axis=1, keepdims=True), mcr)
            e = jnp.exp(s - jnp.concatenate([m, m], axis=1))
            f = jnp.exp(mcr - m)
            inv = 1.0 / (jnp.sum(e, axis=1, keepdims=True) + per_row(lcs) * f)
            nc = jnp.concatenate(
                [jnp.broadcast_to(ncs[2 * b + t : 2 * b + t + 1, lanes], (BLOCK, 128)) for t in (0, 1, 0, 1)],
                axis=0,
            )
            num = dot(e.astype(BF16), vext[win, lanes]) + nc * f
            att_ref[mine, lanes] = choose(num * inv).astype(BF16)
            e_ref[u] = e
            inv_ref[u] = inv
            wt_ref[u] = f * inv
        return carry

    lax.fori_loop(0, pairs, forward, 0)

    mixed_ref[...] = dot(att_ref[...], w_ref[...]).astype(BF16)
    gw_ref[...] = dot_tn(att_ref[...], c_ref[...])

    dke[...] = jnp.zeros_like(dke)
    dve[...] = jnp.zeros_like(dve)

    def backward(p, carry):
        lanes = pl.ds(pl.multiple_of(p * 128, 128), 128)
        for b in range(halves):
            u = p * halves + b
            mine, win = pl.ds(128 * b, 128), pl.ds(128 * b, 256)
            q2 = stack(q_ref[mine, lanes] * scale)
            d2 = stack(da_ref[mine, lanes])
            att = att_ref[mine, lanes].astype(F32)
            d2f = d2.astype(F32)
            prod = d2f * jnp.concatenate([att, att], axis=0)
            delta = jnp.sum(prod, axis=1, keepdims=True)
            inv = inv_ref[u]
            pr = e_ref[u] * jnp.concatenate([inv, inv], axis=1)
            kw = kext[win, lanes]
            ds = (pr * (dot_nt(d2, vext[win, lanes]) - delta)).astype(BF16)
            gqa[mine, lanes] = choose(dot(ds, kw)) * scale
            dke[win, lanes] += dot_tn(ds, q2)
            dve[win, lanes] += dot_tn(pr.astype(BF16), d2)
            wt = wt_ref[u]
            for ref, x in ((g_ref, wt * d2f), (h_ref, wt * prod)):
                x = x[:128] + x[128:]
                for t in range(2):
                    ref[2 * b + t : 2 * b + t + 1, lanes] = jnp.sum(
                        x[t * BLOCK : (t + 1) * BLOCK], axis=0, keepdims=True
                    )
        return carry

    lax.fori_loop(0, pairs, backward, 0)

    hs[0] = dke[rows + BLOCK :].astype(BF16)
    hs[1] = dve[rows + BLOCK :].astype(BF16)
    hs[2] = dke[0:BLOCK].astype(BF16)
    hs[3] = dve[0:BLOCK].astype(BF16)
    edge_right = [remote(hs.at[i], hr.at[i], edge_send.at[i], edge_recv.at[i], right) for i in (0, 1)]
    edge_left = [remote(hs.at[i], hr.at[i], edge_send.at[i], edge_recv.at[i], left) for i in (2, 3)]

    @pl.when(has_right)
    def _():
        for copy in edge_right:
            copy.start()

    @pl.when(has_left)
    def _():
        for copy in edge_left:
            copy.start()

    def spread(ref):
        x = jnp.concatenate(
            [jnp.broadcast_to(ref[t : t + 1, :], (heads, hidden)) for t in range(blocks)], axis=0
        )
        return jnp.where(head_mask, x, 0.0)

    gx = spread(g_ref).astype(BF16)
    hsum = jnp.sum(spread(h_ref), axis=1, keepdims=True)
    ds = ec[...] * (pltpu.roll(dot_nt(gx, coarse), cols - 8, 1) - hsum)
    grad = dot_tn(er[...], gx)
    mix = jnp.zeros((hr_rows, cols), F32)
    a_id, b_id = iota((hr_rows, hr_rows), 0), iota((hr_rows, hr_rows), 1)
    for level, width in enumerate(widths):
        dsl = jnp.where(allowed[level], ds, 0.0).astype(BF16)
        grad = grad + dot_tn(dsl, qx[level])
        span = width // BLOCK * heads
        same = (a_id // span == b_id // span) & (a_id % heads == b_id % heads)
        mix = mix + dot(jnp.where(same, 1.0, 0.0).astype(BF16), dsl) * (scale / math.sqrt(width))
    dcs[...] = grad.astype(BF16).reshape(n, SLOT, hidden)
    for o in range(1, n):
        peer = lax.rem(me + o, n)
        remote(dcs.at[peer], dcr.at[o], back_send.at[o], back_recv.at[o], peer).start()

    for t, row in enumerate(fold_heads(dot(mix.astype(BF16), coarse))):
        part = pl.ds(t * BLOCK, BLOCK)
        gq_ref[part, :] = (gqa[part, :] + row).astype(BF16)

    total = dcs[me].astype(F32)
    for o in range(1, n):
        src = lax.rem(me + n - o, n)
        remote(dcs.at[src], dcr.at[o], back_send.at[o], back_recv.at[o], src).wait_recv()
        total = total + dcr[o].astype(F32)
    total = total * row_scale((SLOT, 1))

    @pl.when(has_left)
    def _():
        for i, acc in ((0, dke), (1, dve)):
            edge_right[i].wait_recv()
            acc[BLOCK : 2 * BLOCK] += hr[i].astype(F32)

    @pl.when(has_right)
    def _():
        for i, acc in ((0, dke), (1, dve)):
            edge_left[i].wait_recv()
            acc[rows : rows + BLOCK] += hr[2 + i].astype(F32)

    for t in range(blocks):
        part = pl.ds(t * BLOCK, BLOCK)
        for base, acc, out in ((0, dke, gk_ref), (8, dve, gv_ref)):
            row = total[base + t : base + t + 1]
            second = base + first1 + t // 2
            third = base + first2 + t // 4
            row = row + total[second : second + 1] + total[third : third + 1]
            out[part, :] = (acc[pl.ds((t + 1) * BLOCK, BLOCK), :] + row).astype(BF16)

    for o in range(1, n):
        peer = lax.rem(me + o, n)
        remote(pool.at[me], pool.at[me], pool_send.at[o], pool_recv.at[o], peer).wait_send()
        remote(dcs.at[peer], dcr.at[o], back_send.at[o], back_recv.at[o], peer).wait_send()

    @pl.when(has_right)
    def _():
        for copy in to_right + edge_right:
            copy.wait_send()

    @pl.when(has_left)
    def _():
        for copy in to_left + edge_left:
            copy.wait_send()


def on_device(queries, keys, values, out_weight, cotangent):
    n = lax.axis_size("seq")
    rows, hidden = queries.shape[1:]
    span_one, span_two = max(2, n // 8), n // 2
    units = (hidden // 128) * (rows // 128)
    hrows = rows // BLOCK * HEADS
    ext = rows + 2 * BLOCK
    vm = pl.BlockSpec(memory_space=pltpu.VMEM)
    act = jax.ShapeDtypeStruct((rows, hidden), BF16)
    dma = pltpu.SemaphoreType.DMA
    mixed, gw, gq, gk, gv = pl.pallas_call(
        functools.partial(kernel, n, span_one, span_two),
        out_shape=(act, jax.ShapeDtypeStruct((hidden, hidden), F32), act, act, act),
        in_specs=[vm] * 5,
        out_specs=(vm,) * 5,
        scratch_shapes=[
            pltpu.VMEM((ext, hidden), BF16),
            pltpu.VMEM((ext, hidden), BF16),
            pltpu.VMEM((n, SLOT, hidden), BF16),
            pltpu.VMEM((rows, hidden), BF16),
            pltpu.VMEM((rows, hidden), BF16),
            pltpu.VMEM((rows // 128, 256, 256), F32),
            pltpu.VMEM((3, hrows, hidden), BF16),
            pltpu.VMEM((hrows, SLOT * n), F32),
            pltpu.VMEM((hrows, SLOT * n), BF16),
            pltpu.VMEM((hrows, 128), F32),
            pltpu.VMEM((hrows, 128), F32),
            pltpu.VMEM((8, hidden), F32),
            pltpu.VMEM((units, 256, 256), F32),
            pltpu.VMEM((units, 256, 128), F32),
            pltpu.VMEM((units, 256, 128), F32),
            pltpu.VMEM((8, hidden), F32),
            pltpu.VMEM((8, hidden), F32),
            pltpu.VMEM((rows, hidden), F32),
            pltpu.VMEM((ext, hidden), F32),
            pltpu.VMEM((ext, hidden), F32),
            pltpu.VMEM((4, BLOCK, hidden), BF16),
            pltpu.VMEM((4, BLOCK, hidden), BF16),
            pltpu.VMEM((n, SLOT, hidden), BF16),
            pltpu.VMEM((n, SLOT, hidden), BF16),
            dma((n,)), dma((n,)), dma((4,)), dma((4,)), dma((n,)), dma((n,)), dma((4,)), dma((4,)),
        ],
        compiler_params=pltpu.CompilerParams(
            collective_id=0, has_side_effects=True, vmem_limit_bytes=56 * 1024 * 1024
        ),
    )(queries[0], keys[0], values[0], out_weight, cotangent[0])
    gw = lax.psum_scatter(gw, ("dp", "seq"), scatter_dimension=0, tiled=True)
    return mixed[None], gw, gq[None], gk[None], gv[None]


def solution(mesh):
    tokens = P("dp", "seq", None)
    return jax.shard_map(
        on_device,
        mesh=mesh,
        in_specs=(tokens, tokens, tokens, P(), tokens),
        out_specs=(tokens, P(("dp", "seq"), None), tokens, tokens, tokens),
        check_vma=False,
    )
```

```python
import functools
import math

import jax
import jax.numpy as jnp
from jax import lax
from jax.experimental import pallas as pl
from jax.experimental.pallas import tpu as pltpu
from jax.sharding import PartitionSpec as P

HEADS = 16
HEAD_DIM = 64
BLOCK = 64
MASKED = -1e30
SLOT = 16
F32 = jnp.float32
BF16 = jnp.bfloat16


def dot(a, b):
    return lax.dot_general(a, b, (((1,), (0,)), ((), ())), preferred_element_type=F32)


def dot_nt(a, b):
    return lax.dot_general(a, b, (((1,), (1,)), ((), ())), preferred_element_type=F32)


def dot_tn(a, b):
    return lax.dot_general(a, b, (((0,), (0,)), ((), ())), preferred_element_type=F32)


def iota(shape, dim):
    return lax.broadcasted_iota(jnp.int32, shape, dim)


def kernel(
    n, span_one, span_two,
    q_ref, k_ref, v_ref, w_ref, c_ref,
    mixed_ref, gw_ref, gq_ref, gk_ref, gv_ref,
    kext, vext, pool, da_ref, att_ref, bias, qx, ec, er, mcs, lcs, ncs, e_ref, inv_ref, wt_ref,
    g_ref, h_ref, gqa, dke, dve, hs, hr, dcs, dcr,
    gwb, ra, s1, r1, k1, s2, r2, k2, sd, rd,
    pool_send, pool_recv, halo_send, halo_recv, back_send, back_recv, edge_send, edge_recv,
    tree_send, tree_recv, ring_send, ring_recv,
):
    rows, hidden = q_ref.shape
    blocks = rows // BLOCK
    pairs = hidden // 128
    halves = rows // 128
    widths = (BLOCK, 2 * BLOCK, 4 * BLOCK)
    scale = 1.0 / math.sqrt(HEAD_DIM)
    me = lax.axis_index("seq")
    heads = HEADS
    hr_rows = blocks * heads
    has_left, has_right = me > 0, me < n - 1

    barrier = pltpu.get_barrier_semaphore()
    for o in range(1, n):
        pl.semaphore_signal(
            barrier, inc=1, device_id={"seq": lax.rem(me + o, n)}, device_id_type=pl.DeviceIdType.MESH
        )
    dp = lax.axis_index("dp")
    core, side = dp % 2, dp // 2
    mate, across = dp + 1 - 2 * core, lax.rem(dp + 2, 4)
    for peer in (mate, across):
        pl.semaphore_signal(
            barrier, inc=1, device_id={"dp": peer}, device_id_type=pl.DeviceIdType.MESH
        )
    pl.semaphore_wait(barrier, n + 1)

    def remote(src, dst, ssem, rsem, peer, axis="seq"):
        return pltpu.make_async_remote_copy(
            src_ref=src, dst_ref=dst, send_sem=ssem, recv_sem=rsem,
            device_id={axis: peer}, device_id_type=pl.DeviceIdType.MESH,
        )

    own = hidden // 4
    half = hidden // 2
    parity, place = me % 2, me // 2
    twin = me + 1 - 2 * parity
    groups = n // 2
    part_rows = own // n

    def tree(i, src, dst, axis):
        peer = {"core": mate, "x": across, "y": twin}[axis]
        return remote(src, dst, tree_send.at[i], tree_recv.at[i], peer, "seq" if axis == "y" else "dp")

    first_hop = [tree(i, gwb.at[i, 1 - core], ra.at[i], "core") for i in (0, 1)]
    second_hop = [tree(2 + i, s1.at[i], r1.at[i], "xy"[i]) for i in (0, 1)]
    third_hop = [tree(4 + i, s2.at[i], r2.at[i], "yx"[i]) for i in (0, 1)]

    def by_parity(x):
        low = jnp.concatenate(
            [x[2 * j * part_rows : (2 * j + 1) * part_rows] for j in range(groups)], axis=0
        )
        high = jnp.concatenate(
            [x[(2 * j + 1) * part_rows : (2 * j + 2) * part_rows] for j in range(groups)], axis=0
        )
        return jnp.where(parity == 1, high, low), jnp.where(parity == 1, low, high)

    def by_side(low, high):
        return jnp.where(side == 1, high, low), jnp.where(side == 1, low, high)

    def partial_products(c):
        for x in range(2):
            columns = pl.ds(pl.multiple_of((2 * x + c) * own, own), own)
            y = dot_tn(att_ref[:, columns], c_ref[...]).astype(BF16)
            gwb[0, c, x] = y[:, :half]
            gwb[1, c, x] = y[:, half:]

    def start_first():
        partial_products(1 - core)
        for copy in first_hop:
            copy.start()
        partial_products(core)

    def start_second():
        for i in (0, 1):
            first_hop[i].wait_recv()
            low, high = [gwb[i, core, x].astype(F32) + ra[i, x].astype(F32) for x in range(2)]
            if i == 0:
                keep, send = by_side(low, high)
            else:
                keep_low, send_low = by_parity(low)
                keep_high, send_high = by_parity(high)
                keep = jnp.concatenate([keep_low, keep_high], axis=0)
                send = jnp.concatenate([send_low, send_high], axis=0)
            k1[i] = keep
            s1[i] = send.astype(BF16)
            second_hop[i].start()

    def start_third():
        for i in (0, 1):
            second_hop[i].wait_recv()
            x = k1[i] + r1[i].astype(F32)
            keep, send = by_parity(x) if i == 0 else by_side(x[: own // 2], x[own // 2 :])
            k2[i] = keep
            s2[i] = send.astype(BF16)
            third_hop[i].start()

    def last_hop(o, slot, peer):
        return remote(sd.at[slot], rd.at[o], ring_send.at[o], ring_recv.at[o], 2 * peer + parity)

    def start_last():
        for i in (0, 1):
            third_hop[i].wait_recv()
            x = k2[i] + r2[i].astype(F32)
            k2[i] = x
            for j in range(groups):
                sd[j, i * part_rows : (i + 1) * part_rows] = x[
                    j * part_rows : (j + 1) * part_rows
                ].astype(BF16)
        for o in range(1, groups):
            peer = lax.rem(place + o, groups)
            last_hop(o, peer, peer).start()

    def finish_weight():
        mine = pl.ds(pl.multiple_of(place * part_rows, part_rows), part_rows)
        totals = [k2[i, mine] for i in (0, 1)]
        for o in range(1, groups):
            src = lax.rem(place + groups - o, groups)
            last_hop(o, src, src).wait_recv()
            x = rd[o].astype(F32)
            totals = [totals[0] + x[:part_rows], totals[1] + x[part_rows:]]
        gw_ref[:, :half] = totals[0]
        gw_ref[:, half:] = totals[1]
        for o in range(1, groups):
            peer = lax.rem(place + o, groups)
            last_hop(o, peer, peer).wait_send()
        for copy in first_hop + second_hop + third_hop:
            copy.wait_send()

    left = lax.rem(me + n - 1, n)
    right = lax.rem(me + 1, n)
    top = pl.ds(0, BLOCK)
    last = pl.ds(rows - BLOCK, BLOCK)
    bottom = pl.ds(rows + BLOCK, BLOCK)
    to_right = [
        remote(k_ref.at[last], kext.at[top], halo_send.at[0], halo_recv.at[0], right),
        remote(v_ref.at[last], vext.at[top], halo_send.at[1], halo_recv.at[1], right),
    ]
    to_left = [
        remote(k_ref.at[top], kext.at[bottom], halo_send.at[2], halo_recv.at[2], left),
        remote(v_ref.at[top], vext.at[bottom], halo_send.at[3], halo_recv.at[3], left),
    ]

    r_id, i_id = iota((SLOT, rows), 0), iota((SLOT, rows), 1)

    def pick(rid):
        base, hit = 0, jnp.zeros((SLOT, rows), jnp.bool_)
        for width in widths:
            count = rows // width
            inside = jnp.logical_and(rid >= base, rid < base + count)
            hit = jnp.logical_or(hit, jnp.logical_and(inside, i_id // width == rid - base))
            base += count
        return jnp.where(hit, 1.0, 0.0).astype(BF16)

    first1 = rows // widths[0]
    first2 = first1 + rows // widths[1]

    def row_scale(shape):
        rr = iota(shape, 0) % 8
        return jnp.where(
            rr < first1,
            1.0 / math.sqrt(widths[0]),
            jnp.where(rr < first2, 1.0 / math.sqrt(widths[1]), 1.0 / math.sqrt(widths[2])),
        )

    pooled = dot(pick(r_id), k_ref[...]) + dot(pick(r_id - 8), v_ref[...])
    pool[me] = (pooled * row_scale((SLOT, 1))).astype(BF16)

    for o in range(1, n):
        peer = lax.rem(me + o, n)
        remote(pool.at[me], pool.at[me], pool_send.at[o], pool_recv.at[o], peer).start()

    @pl.when(has_right)
    def _():
        for copy in to_right:
            copy.start()

    @pl.when(has_left)
    def _():
        for copy in to_left:
            copy.start()

    kext[BLOCK : BLOCK + rows] = k_ref[...]
    vext[BLOCK : BLOCK + rows] = v_ref[...]

    @pl.when(me == 0)
    def _():
        kext[0:BLOCK] = jnp.zeros((BLOCK, hidden), BF16)
        vext[0:BLOCK] = jnp.zeros((BLOCK, hidden), BF16)

    @pl.when(me == n - 1)
    def _():
        kext[rows + BLOCK :] = jnp.zeros((BLOCK, hidden), BF16)
        vext[rows + BLOCK :] = jnp.zeros((BLOCK, hidden), BF16)

    da_ref[...] = dot_nt(c_ref[...], w_ref[...]).astype(BF16)

    for b in range(halves):
        qb = (iota((256, 256), 0) % 128) // BLOCK + 1
        kb = iota((256, 256), 1) // BLOCK
        ok = jnp.abs(qb - kb) <= 1
        if b == 0:
            ok = jnp.logical_and(ok, jnp.logical_or(kb > 0, has_left))
        if b == halves - 1:
            ok = jnp.logical_and(ok, jnp.logical_or(kb < 3, has_right))
        bias[b] = jnp.where(ok, 0.0, MASKED)

    x_id, xi_id = iota((hr_rows, rows), 0) // heads, iota((hr_rows, rows), 1)
    head_mask = iota((hr_rows, hidden), 1) // HEAD_DIM == iota((hr_rows, hidden), 0) % heads
    for level, width in enumerate(widths):
        hit = xi_id // width == x_id * BLOCK // width
        rows_q = dot(jnp.where(hit, 1.0, 0.0).astype(BF16), q_ref[...]) * (1.0 / math.sqrt(width))
        rows_q = rows_q.astype(BF16).astype(F32) * scale
        qx[level] = jnp.where(head_mask, rows_q, 0.0).astype(BF16)

    cols = SLOT * n
    t_id = iota((hr_rows, cols), 0) // heads
    dev, rr = iota((hr_rows, cols), 1) // SLOT, iota((hr_rows, cols), 1) % SLOT
    same_one = dev // span_one == me // span_one
    same_two = dev // span_two == me // span_two
    gap = jnp.abs(me * first1 + t_id - dev * first1 - rr)
    allowed = (
        same_one & (rr < first1) & (gap > 1),
        same_two & jnp.logical_not(same_one) & (rr >= first1) & (rr < first2),
        jnp.logical_not(same_two) & (rr >= first2) & (rr < first2 + rows // widths[2]),
    )

    for o in range(1, n):
        src = lax.rem(me + n - o, n)
        remote(pool.at[src], pool.at[src], pool_send.at[o], pool_recv.at[o], src).wait_recv()
    coarse = pool[...].reshape(cols, hidden)
    s = jnp.full((hr_rows, cols), MASKED, F32)
    for level in range(3):
        s = jnp.where(allowed[level], dot_nt(qx[level], coarse), s)
    mc = jnp.max(s, axis=1, keepdims=True)
    ex = jnp.where(s > 0.5 * MASKED, jnp.exp(s - mc), 0.0)
    ec[...] = ex
    rolled = pltpu.roll(ex, 8, 1).astype(BF16)
    er[...] = rolled
    mcs[...] = jnp.broadcast_to(mc, (hr_rows, 128))
    lcs[...] = jnp.broadcast_to(jnp.sum(ex, axis=1, keepdims=True), (hr_rows, 128))

    def fold_heads(x):
        x = jnp.where(head_mask, x, 0.0)
        return [jnp.sum(x[t * heads : (t + 1) * heads], axis=0, keepdims=True) for t in range(blocks)]

    for t, row in enumerate(fold_heads(dot(rolled, coarse))):
        ncs[t : t + 1, :] = row

    @pl.when(has_left)
    def _():
        for copy in to_right:
            copy.wait_recv()

    @pl.when(has_right)
    def _():
        for copy in to_left:
            copy.wait_recv()

    low = iota((128, 128), 1) < HEAD_DIM

    def stack(x):
        zero = jnp.zeros_like(x)
        return jnp.concatenate([jnp.where(low, x, zero), jnp.where(low, zero, x)], axis=0)

    def choose(x):
        return jnp.where(low, x[:128], x[128:])

    def forward(p, carry):
        lanes = pl.ds(pl.multiple_of(p * 128, 128), 128)
        for b in range(halves):
            u = p * halves + b
            mine, win = pl.ds(128 * b, 128), pl.ds(128 * b, 256)
            q2 = stack(q_ref[mine, lanes] * scale)
            s = dot_nt(q2, kext[win, lanes]) + bias[b]

            def per_row(ref):
                parts = []
                for h in range(2):
                    for t in (2 * b, 2 * b + 1):
                        row = ref[pl.ds(t * heads + 2 * p + h, 1), :]
                        parts.append(jnp.broadcast_to(row, (BLOCK, 128)))
                return jnp.concatenate(parts, axis=0)

            mcr = per_row(mcs)
            m = jnp.maximum(jnp.max(s, axis=1, keepdims=True), mcr)
            e = jnp.exp(s - jnp.concatenate([m, m], axis=1))
            f = jnp.exp(mcr - m)
            inv = 1.0 / (jnp.sum(e, axis=1, keepdims=True) + per_row(lcs) * f)
            nc = jnp.concatenate(
                [jnp.broadcast_to(ncs[2 * b + t : 2 * b + t + 1, lanes], (BLOCK, 128)) for t in (0, 1, 0, 1)],
                axis=0,
            )
            num = dot(e.astype(BF16), vext[win, lanes]) + nc * f
            att_ref[mine, lanes] = choose(num * inv).astype(BF16)
            e_ref[u] = e
            inv_ref[u] = inv
            wt_ref[u] = f * inv
        return carry

    lax.fori_loop(0, pairs, forward, 0)

    start_first()
    mixed_ref[...] = dot(att_ref[...], w_ref[...]).astype(BF16)

    dke[...] = jnp.zeros_like(dke)
    dve[...] = jnp.zeros_like(dve)

    def backward(p, carry):
        lanes = pl.ds(pl.multiple_of(p * 128, 128), 128)
        for b in range(halves):
            u = p * halves + b
            mine, win = pl.ds(128 * b, 128), pl.ds(128 * b, 256)
            q2 = stack(q_ref[mine, lanes] * scale)
            d2 = stack(da_ref[mine, lanes])
            att = att_ref[mine, lanes].astype(F32)
            d2f = d2.astype(F32)
            prod = d2f * jnp.concatenate([att, att], axis=0)
            delta = jnp.sum(prod, axis=1, keepdims=True)
            inv = inv_ref[u]
            pr = e_ref[u] * jnp.concatenate([inv, inv], axis=1)
            kw = kext[win, lanes]
            ds = (pr * (dot_nt(d2, vext[win, lanes]) - delta)).astype(BF16)
            gqa[mine, lanes] = choose(dot(ds, kw)) * scale
            dke[win, lanes] += dot_tn(ds, q2)
            dve[win, lanes] += dot_tn(pr.astype(BF16), d2)
            wt = wt_ref[u]
            for ref, x in ((g_ref, wt * d2f), (h_ref, wt * prod)):
                x = x[:128] + x[128:]
                for t in range(2):
                    ref[2 * b + t : 2 * b + t + 1, lanes] = jnp.sum(
                        x[t * BLOCK : (t + 1) * BLOCK], axis=0, keepdims=True
                    )
        return carry

    lax.fori_loop(0, pairs // 4, backward, 0)
    start_second()
    lax.fori_loop(pairs // 4, pairs, backward, 0)

    hs[0] = dke[rows + BLOCK :].astype(BF16)
    hs[1] = dve[rows + BLOCK :].astype(BF16)
    hs[2] = dke[0:BLOCK].astype(BF16)
    hs[3] = dve[0:BLOCK].astype(BF16)
    edge_right = [remote(hs.at[i], hr.at[i], edge_send.at[i], edge_recv.at[i], right) for i in (0, 1)]
    edge_left = [remote(hs.at[i], hr.at[i], edge_send.at[i], edge_recv.at[i], left) for i in (2, 3)]

    @pl.when(has_right)
    def _():
        for copy in edge_right:
            copy.start()

    @pl.when(has_left)
    def _():
        for copy in edge_left:
            copy.start()

    start_third()

    def spread(ref):
        x = jnp.concatenate(
            [jnp.broadcast_to(ref[t : t + 1, :], (heads, hidden)) for t in range(blocks)], axis=0
        )
        return jnp.where(head_mask, x, 0.0)

    gx = spread(g_ref).astype(BF16)
    hsum = jnp.sum(spread(h_ref), axis=1, keepdims=True)
    ds = ec[...] * (pltpu.roll(dot_nt(gx, coarse), cols - 8, 1) - hsum)
    grad = dot_tn(er[...], gx)
    mix = jnp.zeros((hr_rows, cols), F32)
    a_id, b_id = iota((hr_rows, hr_rows), 0), iota((hr_rows, hr_rows), 1)
    for level, width in enumerate(widths):
        dsl = jnp.where(allowed[level], ds, 0.0).astype(BF16)
        grad = grad + dot_tn(dsl, qx[level])
        span = width // BLOCK * heads
        same = (a_id // span == b_id // span) & (a_id % heads == b_id % heads)
        mix = mix + dot(jnp.where(same, 1.0, 0.0).astype(BF16), dsl) * (scale / math.sqrt(width))
    dcs[...] = grad.astype(BF16).reshape(n, SLOT, hidden)
    for o in range(1, n):
        peer = lax.rem(me + o, n)
        remote(dcs.at[peer], dcr.at[o], back_send.at[o], back_recv.at[o], peer).start()

    for t, row in enumerate(fold_heads(dot(mix.astype(BF16), coarse))):
        part = pl.ds(t * BLOCK, BLOCK)
        gq_ref[part, :] = (gqa[part, :] + row).astype(BF16)

    start_last()
    total = dcs[me].astype(F32)
    for o in range(1, n):
        src = lax.rem(me + n - o, n)
        remote(dcs.at[src], dcr.at[o], back_send.at[o], back_recv.at[o], src).wait_recv()
        total = total + dcr[o].astype(F32)
    total = total * row_scale((SLOT, 1))

    @pl.when(has_left)
    def _():
        for i, acc in ((0, dke), (1, dve)):
            edge_right[i].wait_recv()
            acc[BLOCK : 2 * BLOCK] += hr[i].astype(F32)

    @pl.when(has_right)
    def _():
        for i, acc in ((0, dke), (1, dve)):
            edge_left[i].wait_recv()
            acc[rows : rows + BLOCK] += hr[2 + i].astype(F32)

    for t in range(blocks):
        part = pl.ds(t * BLOCK, BLOCK)
        for base, acc, out in ((0, dke, gk_ref), (8, dve, gv_ref)):
            row = total[base + t : base + t + 1]
            second = base + first1 + t // 2
            third = base + first2 + t // 4
            row = row + total[second : second + 1] + total[third : third + 1]
            out[part, :] = (acc[pl.ds((t + 1) * BLOCK, BLOCK), :] + row).astype(BF16)

    finish_weight()
    for o in range(1, n):
        peer = lax.rem(me + o, n)
        remote(pool.at[me], pool.at[me], pool_send.at[o], pool_recv.at[o], peer).wait_send()
        remote(dcs.at[peer], dcr.at[o], back_send.at[o], back_recv.at[o], peer).wait_send()

    @pl.when(has_right)
    def _():
        for copy in to_right + edge_right:
            copy.wait_send()

    @pl.when(has_left)
    def _():
        for copy in to_left + edge_left:
            copy.wait_send()


def on_device(queries, keys, values, out_weight, cotangent):
    n = lax.axis_size("seq")
    rows, hidden = queries.shape[1:]
    span_one, span_two = max(2, n // 8), n // 2
    units = (hidden // 128) * (rows // 128)
    hrows = rows // BLOCK * HEADS
    ext = rows + 2 * BLOCK
    vm = pl.BlockSpec(memory_space=pltpu.VMEM)
    own, half = hidden // 4, hidden // 2
    act = jax.ShapeDtypeStruct((rows, hidden), BF16)
    dma = pltpu.SemaphoreType.DMA
    mixed, gw, gq, gk, gv = pl.pallas_call(
        functools.partial(kernel, n, span_one, span_two),
        out_shape=(act, jax.ShapeDtypeStruct((own // n, hidden), F32), act, act, act),
        in_specs=[vm] * 5,
        out_specs=(vm,) * 5,
        scratch_shapes=[
            pltpu.VMEM((ext, hidden), BF16),
            pltpu.VMEM((ext, hidden), BF16),
            pltpu.VMEM((n, SLOT, hidden), BF16),
            pltpu.VMEM((rows, hidden), BF16),
            pltpu.VMEM((rows, hidden), BF16),
            pltpu.VMEM((rows // 128, 256, 256), F32),
            pltpu.VMEM((3, hrows, hidden), BF16),
            pltpu.VMEM((hrows, SLOT * n), F32),
            pltpu.VMEM((hrows, SLOT * n), BF16),
            pltpu.VMEM((hrows, 128), F32),
            pltpu.VMEM((hrows, 128), F32),
            pltpu.VMEM((8, hidden), F32),
            pltpu.VMEM((units, 256, 256), F32),
            pltpu.VMEM((units, 256, 128), F32),
            pltpu.VMEM((units, 256, 128), F32),
            pltpu.VMEM((8, hidden), F32),
            pltpu.VMEM((8, hidden), F32),
            pltpu.VMEM((rows, hidden), F32),
            pltpu.VMEM((ext, hidden), F32),
            pltpu.VMEM((ext, hidden), F32),
            pltpu.VMEM((4, BLOCK, hidden), BF16),
            pltpu.VMEM((4, BLOCK, hidden), BF16),
            pltpu.VMEM((n, SLOT, hidden), BF16),
            pltpu.VMEM((n, SLOT, hidden), BF16),
            pltpu.VMEM((2, 2, 2, own, half), BF16),
            pltpu.VMEM((2, 2, own, half), BF16),
            pltpu.VMEM((2, own, half), BF16),
            pltpu.VMEM((2, own, half), BF16),
            pltpu.VMEM((2, own, half), F32),
            pltpu.VMEM((2, own // 2, half), BF16),
            pltpu.VMEM((2, own // 2, half), BF16),
            pltpu.VMEM((2, own // 2, half), F32),
            pltpu.VMEM((n // 2, 2 * own // n, half), BF16),
            pltpu.VMEM((n // 2, 2 * own // n, half), BF16),
            dma((n,)), dma((n,)), dma((4,)), dma((4,)), dma((n,)), dma((n,)), dma((4,)), dma((4,)),
            dma((6,)), dma((6,)), dma((n // 2,)), dma((n // 2,)),
        ],
        compiler_params=pltpu.CompilerParams(
            collective_id=0, has_side_effects=True, vmem_limit_bytes=56 * 1024 * 1024
        ),
    )(queries[0], keys[0], values[0], out_weight, cotangent[0])
    return mixed[None], gw, gq[None], gk[None], gv[None]


def solution(mesh):
    tokens = P("dp", "seq", None)
    return jax.shard_map(
        on_device,
        mesh=mesh,
        in_specs=(tokens, tokens, tokens, P(), tokens),
        out_specs=(tokens, P(("dp", "seq"), None), tokens, tokens, tokens),
        check_vma=False,
    )
```

```python
import functools
import math

import jax
import jax.numpy as jnp
from jax import lax
from jax.experimental import pallas as pl
from jax.experimental.pallas import tpu as pltpu
from jax.sharding import PartitionSpec as P

HEADS = 16
HEAD_DIM = 64
BLOCK = 64
MASKED = -1e30
SLOT = 16
F32 = jnp.float32
BF16 = jnp.bfloat16


def dot(a, b):
    return lax.dot_general(a, b, (((1,), (0,)), ((), ())), preferred_element_type=F32)


def dot_nt(a, b):
    return lax.dot_general(a, b, (((1,), (1,)), ((), ())), preferred_element_type=F32)


def dot_tn(a, b):
    return lax.dot_general(a, b, (((0,), (0,)), ((), ())), preferred_element_type=F32)


def iota(shape, dim):
    return lax.broadcasted_iota(jnp.int32, shape, dim)


def kernel(
    n, span_one, span_two,
    q_ref, k_ref, v_ref, w_ref, c_ref,
    mixed_ref, gw_ref, gq_ref, gk_ref, gv_ref,
    kext, vext, pool, da_ref, att_ref, bias, qx, ec, er, mcs, lcs, ncs, e_ref, inv_ref, wt_ref,
    g_ref, h_ref, gqa, dke, dve, hs, hr, dcs, dcr,
    gwb, ra, s1, r1, k1, s2, r2, k2, sd, rd,
    pool_send, pool_recv, halo_send, halo_recv, back_send, back_recv, edge_send, edge_recv,
    tree_send, tree_recv, ring_send, ring_recv,
):
    rows, hidden = q_ref.shape
    blocks = rows // BLOCK
    pairs = hidden // 128
    halves = rows // 128
    widths = (BLOCK, 2 * BLOCK, 4 * BLOCK)
    scale = 1.0 / math.sqrt(HEAD_DIM)
    me = lax.axis_index("seq")
    heads = HEADS
    hr_rows = blocks * heads
    has_left, has_right = me > 0, me < n - 1

    barrier = pltpu.get_barrier_semaphore()
    for o in range(1, n):
        pl.semaphore_signal(
            barrier, inc=1, device_id={"seq": lax.rem(me + o, n)}, device_id_type=pl.DeviceIdType.MESH
        )
    dp = lax.axis_index("dp")
    core, side = dp % 2, dp // 2
    mate, across = dp + 1 - 2 * core, lax.rem(dp + 2, 4)
    for peer in (mate, across):
        pl.semaphore_signal(
            barrier, inc=1, device_id={"dp": peer}, device_id_type=pl.DeviceIdType.MESH
        )
    pl.semaphore_wait(barrier, n + 1)

    def remote(src, dst, ssem, rsem, peer, axis="seq"):
        return pltpu.make_async_remote_copy(
            src_ref=src, dst_ref=dst, send_sem=ssem, recv_sem=rsem,
            device_id={axis: peer}, device_id_type=pl.DeviceIdType.MESH,
        )

    own = hidden // 4
    half = hidden // 2
    parity, place = me % 2, me // 2
    twin = me + 1 - 2 * parity
    groups = n // 2
    part_rows = own // n

    def tree(i, src, dst, axis):
        peer = {"core": mate, "x": across, "y": twin}[axis]
        return remote(src, dst, tree_send.at[i], tree_recv.at[i], peer, "seq" if axis == "y" else "dp")

    first_hop = [tree(i, gwb.at[i, 1 - core], ra.at[i], "core") for i in (0, 1)]
    second_hop = [tree(2 + i, s1.at[i], r1.at[i], "xy"[i]) for i in (0, 1)]
    third_hop = [tree(4 + i, s2.at[i], r2.at[i], "yx"[i]) for i in (0, 1)]

    def by_parity(x):
        low = jnp.concatenate(
            [x[2 * j * part_rows : (2 * j + 1) * part_rows] for j in range(groups)], axis=0
        )
        high = jnp.concatenate(
            [x[(2 * j + 1) * part_rows : (2 * j + 2) * part_rows] for j in range(groups)], axis=0
        )
        return jnp.where(parity == 1, high, low), jnp.where(parity == 1, low, high)

    def by_side(low, high):
        return jnp.where(side == 1, high, low), jnp.where(side == 1, low, high)

    def partial_products(c):
        for x in range(2):
            columns = pl.ds(pl.multiple_of((2 * x + c) * own, own), own)
            y = dot_tn(att_ref[:, columns], c_ref[...]).astype(BF16)
            gwb[0, c, x] = y[:, :half]
            gwb[1, c, x] = y[:, half:]

    def start_first():
        partial_products(1 - core)
        for copy in first_hop:
            copy.start()
        partial_products(core)

    def start_second():
        for i in (0, 1):
            first_hop[i].wait_recv()
            low, high = [gwb[i, core, x].astype(F32) + ra[i, x].astype(F32) for x in range(2)]
            if i == 0:
                keep, send = by_side(low, high)
            else:
                keep_low, send_low = by_parity(low)
                keep_high, send_high = by_parity(high)
                keep = jnp.concatenate([keep_low, keep_high], axis=0)
                send = jnp.concatenate([send_low, send_high], axis=0)
            k1[i] = keep
            s1[i] = send.astype(BF16)
            second_hop[i].start()

    def start_third():
        for i in (0, 1):
            second_hop[i].wait_recv()
            x = k1[i] + r1[i].astype(F32)
            keep, send = by_parity(x) if i == 0 else by_side(x[: own // 2], x[own // 2 :])
            k2[i] = keep
            s2[i] = send.astype(BF16)
            third_hop[i].start()

    def last_hop(o, slot, peer):
        return remote(sd.at[slot], rd.at[o], ring_send.at[o], ring_recv.at[o], 2 * peer + parity)

    def start_last():
        for i in (0, 1):
            third_hop[i].wait_recv()
            x = k2[i] + r2[i].astype(F32)
            k2[i] = x
            for j in range(groups):
                sd[j, i * part_rows : (i + 1) * part_rows] = x[
                    j * part_rows : (j + 1) * part_rows
                ].astype(BF16)
        for o in range(1, groups):
            peer = lax.rem(place + o, groups)
            last_hop(o, peer, peer).start()

    def finish_weight():
        mine = pl.ds(pl.multiple_of(place * part_rows, part_rows), part_rows)
        totals = [k2[i, mine] for i in (0, 1)]
        for o in range(1, groups):
            src = lax.rem(place + groups - o, groups)
            last_hop(o, src, src).wait_recv()
            x = rd[o].astype(F32)
            totals = [totals[0] + x[:part_rows], totals[1] + x[part_rows:]]
        gw_ref[:, :half] = totals[0]
        gw_ref[:, half:] = totals[1]
        for o in range(1, groups):
            peer = lax.rem(place + o, groups)
            last_hop(o, peer, peer).wait_send()
        for copy in first_hop + second_hop + third_hop:
            copy.wait_send()

    left = lax.rem(me + n - 1, n)
    right = lax.rem(me + 1, n)
    top = pl.ds(0, BLOCK)
    last = pl.ds(rows - BLOCK, BLOCK)
    bottom = pl.ds(rows + BLOCK, BLOCK)
    to_right = [
        remote(k_ref.at[last], kext.at[top], halo_send.at[0], halo_recv.at[0], right),
        remote(v_ref.at[last], vext.at[top], halo_send.at[1], halo_recv.at[1], right),
    ]
    to_left = [
        remote(k_ref.at[top], kext.at[bottom], halo_send.at[2], halo_recv.at[2], left),
        remote(v_ref.at[top], vext.at[bottom], halo_send.at[3], halo_recv.at[3], left),
    ]

    r_id, i_id = iota((SLOT, rows), 0), iota((SLOT, rows), 1)

    def pick(rid):
        base, hit = 0, jnp.zeros((SLOT, rows), jnp.bool_)
        for width in widths:
            count = rows // width
            inside = jnp.logical_and(rid >= base, rid < base + count)
            hit = jnp.logical_or(hit, jnp.logical_and(inside, i_id // width == rid - base))
            base += count
        return jnp.where(hit, 1.0, 0.0).astype(BF16)

    first1 = rows // widths[0]
    first2 = first1 + rows // widths[1]

    def row_scale(shape):
        rr = iota(shape, 0) % 8
        return jnp.where(
            rr < first1,
            1.0 / math.sqrt(widths[0]),
            jnp.where(rr < first2, 1.0 / math.sqrt(widths[1]), 1.0 / math.sqrt(widths[2])),
        )

    pooled = dot(pick(r_id), k_ref[...]) + dot(pick(r_id - 8), v_ref[...])
    pool[me] = (pooled * row_scale((SLOT, 1))).astype(BF16)

    for o in range(1, n):
        peer = lax.rem(me + o, n)
        remote(pool.at[me], pool.at[me], pool_send.at[o], pool_recv.at[o], peer).start()

    @pl.when(has_right)
    def _():
        for copy in to_right:
            copy.start()

    @pl.when(has_left)
    def _():
        for copy in to_left:
            copy.start()

    kext[BLOCK : BLOCK + rows] = k_ref[...]
    vext[BLOCK : BLOCK + rows] = v_ref[...]

    @pl.when(me == 0)
    def _():
        kext[0:BLOCK] = jnp.zeros((BLOCK, hidden), BF16)
        vext[0:BLOCK] = jnp.zeros((BLOCK, hidden), BF16)

    @pl.when(me == n - 1)
    def _():
        kext[rows + BLOCK :] = jnp.zeros((BLOCK, hidden), BF16)
        vext[rows + BLOCK :] = jnp.zeros((BLOCK, hidden), BF16)

    da_ref[...] = dot_nt(c_ref[...], w_ref[...]).astype(BF16)

    for b in range(halves):
        qb = (iota((256, 256), 0) % 128) // BLOCK + 1
        kb = iota((256, 256), 1) // BLOCK
        ok = jnp.abs(qb - kb) <= 1
        if b == 0:
            ok = jnp.logical_and(ok, jnp.logical_or(kb > 0, has_left))
        if b == halves - 1:
            ok = jnp.logical_and(ok, jnp.logical_or(kb < 3, has_right))
        bias[b] = jnp.where(ok, 0.0, MASKED)

    x_id, xi_id = iota((hr_rows, rows), 0) // heads, iota((hr_rows, rows), 1)
    head_mask = iota((hr_rows, hidden), 1) // HEAD_DIM == iota((hr_rows, hidden), 0) % heads
    for level, width in enumerate(widths):
        hit = xi_id // width == x_id * BLOCK // width
        rows_q = dot(jnp.where(hit, 1.0, 0.0).astype(BF16), q_ref[...]) * (1.0 / math.sqrt(width))
        rows_q = rows_q.astype(BF16).astype(F32) * scale
        qx[level] = jnp.where(head_mask, rows_q, 0.0).astype(BF16)

    cols = SLOT * n
    t_id = iota((hr_rows, cols), 0) // heads
    dev, rr = iota((hr_rows, cols), 1) // SLOT, iota((hr_rows, cols), 1) % SLOT
    same_one = dev // span_one == me // span_one
    same_two = dev // span_two == me // span_two
    gap = jnp.abs(me * first1 + t_id - dev * first1 - rr)
    allowed = (
        same_one & (rr < first1) & (gap > 1),
        same_two & jnp.logical_not(same_one) & (rr >= first1) & (rr < first2),
        jnp.logical_not(same_two) & (rr >= first2) & (rr < first2 + rows // widths[2]),
    )

    for o in range(1, n):
        src = lax.rem(me + n - o, n)
        remote(pool.at[src], pool.at[src], pool_send.at[o], pool_recv.at[o], src).wait_recv()
    coarse = pool[...].reshape(cols, hidden)
    s = jnp.full((hr_rows, cols), MASKED, F32)
    for level in range(3):
        s = jnp.where(allowed[level], dot_nt(qx[level], coarse), s)
    mc = jnp.max(s, axis=1, keepdims=True)
    ex = jnp.where(s > 0.5 * MASKED, jnp.exp(s - mc), 0.0)
    ec[...] = ex
    rolled = pltpu.roll(ex, 8, 1).astype(BF16)
    er[...] = rolled
    mcs[...] = jnp.broadcast_to(mc, (hr_rows, 128))
    lcs[...] = jnp.broadcast_to(jnp.sum(ex, axis=1, keepdims=True), (hr_rows, 128))

    def fold_heads(x):
        x = jnp.where(head_mask, x, 0.0)
        return [jnp.sum(x[t * heads : (t + 1) * heads], axis=0, keepdims=True) for t in range(blocks)]

    for t, row in enumerate(fold_heads(dot(rolled, coarse))):
        ncs[t : t + 1, :] = row

    @pl.when(has_left)
    def _():
        for copy in to_right:
            copy.wait_recv()

    @pl.when(has_right)
    def _():
        for copy in to_left:
            copy.wait_recv()

    low = iota((128, 128), 1) < HEAD_DIM

    def stack(x):
        zero = jnp.zeros_like(x)
        return jnp.concatenate([jnp.where(low, x, zero), jnp.where(low, zero, x)], axis=0)

    def choose(x):
        return jnp.where(low, x[:128], x[128:])

    def forward(p):
        lanes = pl.ds(pl.multiple_of(p * 128, 128), 128)
        for b in range(halves):
            u = p * halves + b
            mine, win = pl.ds(128 * b, 128), pl.ds(128 * b, 256)
            q2 = stack(q_ref[mine, lanes] * scale)
            s = dot_nt(q2, kext[win, lanes]) + bias[b]

            def per_row(ref):
                parts = []
                for h in range(2):
                    for t in (2 * b, 2 * b + 1):
                        row = ref[pl.ds(t * heads + 2 * p + h, 1), :]
                        parts.append(jnp.broadcast_to(row, (BLOCK, 128)))
                return jnp.concatenate(parts, axis=0)

            mcr = per_row(mcs)
            m = jnp.maximum(jnp.max(s, axis=1, keepdims=True), mcr)
            e = jnp.exp(s - jnp.concatenate([m, m], axis=1))
            f = jnp.exp(mcr - m)
            inv = 1.0 / (jnp.sum(e, axis=1, keepdims=True) + per_row(lcs) * f)
            nc = jnp.concatenate(
                [jnp.broadcast_to(ncs[2 * b + t : 2 * b + t + 1, lanes], (BLOCK, 128)) for t in (0, 1, 0, 1)],
                axis=0,
            )
            num = dot(e.astype(BF16), vext[win, lanes]) + nc * f
            att_ref[mine, lanes] = choose(num * inv).astype(BF16)
            e_ref[u] = e
            inv_ref[u] = inv
            wt_ref[u] = f * inv

    def in_twos(step, first, stop):
        def body(i, carry):
            step(2 * i)
            step(2 * i + 1)
            return carry

        lax.fori_loop(first // 2, stop // 2, body, 0)

    in_twos(forward, 0, pairs)

    start_first()
    mixed_ref[...] = dot(att_ref[...], w_ref[...]).astype(BF16)

    def backward(p):
        lanes = pl.ds(pl.multiple_of(p * 128, 128), 128)
        carried = None
        for b in range(halves):
            u = p * halves + b
            mine, win = pl.ds(128 * b, 128), pl.ds(128 * b, 256)
            q2 = stack(q_ref[mine, lanes] * scale)
            d2 = stack(da_ref[mine, lanes])
            att = att_ref[mine, lanes].astype(F32)
            d2f = d2.astype(F32)
            prod = d2f * jnp.concatenate([att, att], axis=0)
            delta = jnp.sum(prod, axis=1, keepdims=True)
            inv = inv_ref[u]
            pr = e_ref[u] * jnp.concatenate([inv, inv], axis=1)
            kw = kext[win, lanes]
            ds = (pr * (dot_nt(d2, vext[win, lanes]) - delta)).astype(BF16)
            gqa[mine, lanes] = choose(dot(ds, kw)) * scale
            grads = [dot_tn(ds, q2), dot_tn(pr.astype(BF16), d2)]
            for i, acc in enumerate((dke, dve)):
                head = grads[i][:128] if b == 0 else grads[i][:128] + carried[i]
                acc[mine, lanes] = head
                if b == halves - 1:
                    acc[pl.ds(128 * (b + 1), 128), lanes] = grads[i][128:]
            carried = [x[128:] for x in grads]
            wt = wt_ref[u]
            for ref, x in ((g_ref, wt * d2f), (h_ref, wt * prod)):
                x = x[:128] + x[128:]
                for t in range(2):
                    ref[2 * b + t : 2 * b + t + 1, lanes] = jnp.sum(
                        x[t * BLOCK : (t + 1) * BLOCK], axis=0, keepdims=True
                    )

    in_twos(backward, 0, pairs // 4)
    start_second()
    in_twos(backward, pairs // 4, 3 * pairs // 4)
    start_third()
    in_twos(backward, 3 * pairs // 4, pairs)

    hs[0] = dke[rows + BLOCK :].astype(BF16)
    hs[1] = dve[rows + BLOCK :].astype(BF16)
    hs[2] = dke[0:BLOCK].astype(BF16)
    hs[3] = dve[0:BLOCK].astype(BF16)
    edge_right = [remote(hs.at[i], hr.at[i], edge_send.at[i], edge_recv.at[i], right) for i in (0, 1)]
    edge_left = [remote(hs.at[i], hr.at[i], edge_send.at[i], edge_recv.at[i], left) for i in (2, 3)]

    @pl.when(has_right)
    def _():
        for copy in edge_right:
            copy.start()

    @pl.when(has_left)
    def _():
        for copy in edge_left:
            copy.start()

    start_last()

    def spread(ref):
        x = jnp.concatenate(
            [jnp.broadcast_to(ref[t : t + 1, :], (heads, hidden)) for t in range(blocks)], axis=0
        )
        return jnp.where(head_mask, x, 0.0)

    gx = spread(g_ref).astype(BF16)
    hsum = jnp.sum(spread(h_ref), axis=1, keepdims=True)
    ds = ec[...] * (pltpu.roll(dot_nt(gx, coarse), cols - 8, 1) - hsum)
    grad = dot_tn(er[...], gx)
    mix = jnp.zeros((hr_rows, cols), F32)
    a_id, b_id = iota((hr_rows, hr_rows), 0), iota((hr_rows, hr_rows), 1)
    for level, width in enumerate(widths):
        dsl = jnp.where(allowed[level], ds, 0.0).astype(BF16)
        grad = grad + dot_tn(dsl, qx[level])
        span = width // BLOCK * heads
        same = (a_id // span == b_id // span) & (a_id % heads == b_id % heads)
        mix = mix + dot(jnp.where(same, 1.0, 0.0).astype(BF16), dsl) * (scale / math.sqrt(width))
    dcs[...] = grad.astype(BF16).reshape(n, SLOT, hidden)
    for o in range(1, n):
        peer = lax.rem(me + o, n)
        remote(dcs.at[peer], dcr.at[o], back_send.at[o], back_recv.at[o], peer).start()

    for t, row in enumerate(fold_heads(dot(mix.astype(BF16), coarse))):
        part = pl.ds(t * BLOCK, BLOCK)
        gq_ref[part, :] = (gqa[part, :] + row).astype(BF16)

    total = dcs[me].astype(F32)
    for o in range(1, n):
        src = lax.rem(me + n - o, n)
        remote(dcs.at[src], dcr.at[o], back_send.at[o], back_recv.at[o], src).wait_recv()
        total = total + dcr[o].astype(F32)
    total = total * row_scale((SLOT, 1))

    @pl.when(has_left)
    def _():
        for i, acc in ((0, dke), (1, dve)):
            edge_right[i].wait_recv()
            acc[BLOCK : 2 * BLOCK] += hr[i].astype(F32)

    @pl.when(has_right)
    def _():
        for i, acc in ((0, dke), (1, dve)):
            edge_left[i].wait_recv()
            acc[rows : rows + BLOCK] += hr[2 + i].astype(F32)

    for t in range(blocks):
        part = pl.ds(t * BLOCK, BLOCK)
        for base, acc, out in ((0, dke, gk_ref), (8, dve, gv_ref)):
            row = total[base + t : base + t + 1]
            second = base + first1 + t // 2
            third = base + first2 + t // 4
            row = row + total[second : second + 1] + total[third : third + 1]
            out[part, :] = (acc[pl.ds((t + 1) * BLOCK, BLOCK), :] + row).astype(BF16)

    finish_weight()
    for o in range(1, n):
        peer = lax.rem(me + o, n)
        remote(pool.at[me], pool.at[me], pool_send.at[o], pool_recv.at[o], peer).wait_send()
        remote(dcs.at[peer], dcr.at[o], back_send.at[o], back_recv.at[o], peer).wait_send()

    @pl.when(has_right)
    def _():
        for copy in to_right + edge_right:
            copy.wait_send()

    @pl.when(has_left)
    def _():
        for copy in to_left + edge_left:
            copy.wait_send()


def on_device(queries, keys, values, out_weight, cotangent):
    n = lax.axis_size("seq")
    rows, hidden = queries.shape[1:]
    span_one, span_two = max(2, n // 8), n // 2
    units = (hidden // 128) * (rows // 128)
    hrows = rows // BLOCK * HEADS
    ext = rows + 2 * BLOCK
    vm = pl.BlockSpec(memory_space=pltpu.VMEM)
    own, half = hidden // 4, hidden // 2
    act = jax.ShapeDtypeStruct((rows, hidden), BF16)
    dma = pltpu.SemaphoreType.DMA
    mixed, gw, gq, gk, gv = pl.pallas_call(
        functools.partial(kernel, n, span_one, span_two),
        out_shape=(act, jax.ShapeDtypeStruct((own // n, hidden), F32), act, act, act),
        in_specs=[vm] * 5,
        out_specs=(vm,) * 5,
        scratch_shapes=[
            pltpu.VMEM((ext, hidden), BF16),
            pltpu.VMEM((ext, hidden), BF16),
            pltpu.VMEM((n, SLOT, hidden), BF16),
            pltpu.VMEM((rows, hidden), BF16),
            pltpu.VMEM((rows, hidden), BF16),
            pltpu.VMEM((rows // 128, 256, 256), F32),
            pltpu.VMEM((3, hrows, hidden), BF16),
            pltpu.VMEM((hrows, SLOT * n), F32),
            pltpu.VMEM((hrows, SLOT * n), BF16),
            pltpu.VMEM((hrows, 128), F32),
            pltpu.VMEM((hrows, 128), F32),
            pltpu.VMEM((8, hidden), F32),
            pltpu.VMEM((units, 256, 256), F32),
            pltpu.VMEM((units, 256, 128), F32),
            pltpu.VMEM((units, 256, 128), F32),
            pltpu.VMEM((8, hidden), F32),
            pltpu.VMEM((8, hidden), F32),
            pltpu.VMEM((rows, hidden), F32),
            pltpu.VMEM((ext, hidden), F32),
            pltpu.VMEM((ext, hidden), F32),
            pltpu.VMEM((4, BLOCK, hidden), BF16),
            pltpu.VMEM((4, BLOCK, hidden), BF16),
            pltpu.VMEM((n, SLOT, hidden), BF16),
            pltpu.VMEM((n, SLOT, hidden), BF16),
            pltpu.VMEM((2, 2, 2, own, half), BF16),
            pltpu.VMEM((2, 2, own, half), BF16),
            pltpu.VMEM((2, own, half), BF16),
            pltpu.VMEM((2, own, half), BF16),
            pltpu.VMEM((2, own, half), F32),
            pltpu.VMEM((2, own // 2, half), BF16),
            pltpu.VMEM((2, own // 2, half), BF16),
            pltpu.VMEM((2, own // 2, half), F32),
            pltpu.VMEM((n // 2, 2 * own // n, half), BF16),
            pltpu.VMEM((n // 2, 2 * own // n, half), BF16),
            dma((n,)), dma((n,)), dma((4,)), dma((4,)), dma((n,)), dma((n,)), dma((4,)), dma((4,)),
            dma((6,)), dma((6,)), dma((n // 2,)), dma((n // 2,)),
        ],
        compiler_params=pltpu.CompilerParams(
            collective_id=0, has_side_effects=True, vmem_limit_bytes=56 * 1024 * 1024
        ),
    )(queries[0], keys[0], values[0], out_weight, cotangent[0])
    return mixed[None], gw, gq[None], gk[None], gv[None]


def solution(mesh):
    tokens = P("dp", "seq", None)
    return jax.shard_map(
        on_device,
        mesh=mesh,
        in_specs=(tokens, tokens, tokens, P(), tokens),
        out_specs=(tokens, P(("dp", "seq"), None), tokens, tokens, tokens),
        check_vma=False,
    )
```

```python
import functools
import math

import jax
import jax.numpy as jnp
from jax import lax
from jax.experimental import pallas as pl
from jax.experimental.pallas import tpu as pltpu
from jax.sharding import PartitionSpec as P

HEADS = 16
HEAD_DIM = 64
BLOCK = 64
MASKED = -1e30
SLOT = 16
F32 = jnp.float32
BF16 = jnp.bfloat16


def dot(a, b):
    return lax.dot_general(a, b, (((1,), (0,)), ((), ())), preferred_element_type=F32)


def dot_nt(a, b):
    return lax.dot_general(a, b, (((1,), (1,)), ((), ())), preferred_element_type=F32)


def dot_tn(a, b):
    return lax.dot_general(a, b, (((0,), (0,)), ((), ())), preferred_element_type=F32)


def iota(shape, dim):
    return lax.broadcasted_iota(jnp.int32, shape, dim)


def kernel(
    n, span_one, span_two,
    q_ref, k_ref, v_ref, w_ref, c_ref,
    mixed_ref, gw_ref, gq_ref, gk_ref, gv_ref,
    kext, vext, pool, da_ref, att_ref, bias, qx, ec, er, mcs, lcs, ncs, e_ref, inv_ref, wt_ref,
    g_ref, h_ref, gqa, dke, dve, hs, hr, dcs, dcr,
    gwb, ra, s1, r1, k1, s2, r2, k2, sd, rd,
    pool_send, pool_recv, halo_send, halo_recv, back_send, back_recv, edge_send, edge_recv,
    tree_send, tree_recv, ring_send, ring_recv,
):
    rows, hidden = q_ref.shape
    blocks = rows // BLOCK
    pairs = hidden // 128
    halves = rows // 128
    widths = (BLOCK, 2 * BLOCK, 4 * BLOCK)
    scale = 1.0 / math.sqrt(HEAD_DIM)
    me = lax.axis_index("seq")
    heads = HEADS
    hr_rows = blocks * heads
    has_left, has_right = me > 0, me < n - 1

    barrier = pltpu.get_barrier_semaphore()
    for o in range(1, n):
        pl.semaphore_signal(
            barrier, inc=1, device_id={"seq": lax.rem(me + o, n)}, device_id_type=pl.DeviceIdType.MESH
        )
    dp = lax.axis_index("dp")
    core, side = dp % 2, dp // 2
    mate, across = dp + 1 - 2 * core, lax.rem(dp + 2, 4)
    for peer in (mate, across):
        pl.semaphore_signal(
            barrier, inc=1, device_id={"dp": peer}, device_id_type=pl.DeviceIdType.MESH
        )
    pl.semaphore_wait(barrier, n + 1)

    def remote(src, dst, ssem, rsem, peer, axis="seq"):
        return pltpu.make_async_remote_copy(
            src_ref=src, dst_ref=dst, send_sem=ssem, recv_sem=rsem,
            device_id={axis: peer}, device_id_type=pl.DeviceIdType.MESH,
        )

    own = hidden // 4
    half = hidden // 2
    parity, place = me % 2, me // 2
    twin = me + 1 - 2 * parity
    groups = n // 2
    part_rows = own // n

    def tree(i, src, dst, axis):
        peer = {"core": mate, "x": across, "y": twin}[axis]
        return remote(src, dst, tree_send.at[i], tree_recv.at[i], peer, "seq" if axis == "y" else "dp")

    first_hop = [tree(i, gwb.at[i, 1 - core], ra.at[i], "core") for i in (0, 1)]
    second_hop = [tree(2 + i, s1.at[i], r1.at[i], "xy"[i]) for i in (0, 1)]
    third_hop = [tree(4 + i, s2.at[i], r2.at[i], "yx"[i]) for i in (0, 1)]

    def by_parity(x):
        low = jnp.concatenate(
            [x[2 * j * part_rows : (2 * j + 1) * part_rows] for j in range(groups)], axis=0
        )
        high = jnp.concatenate(
            [x[(2 * j + 1) * part_rows : (2 * j + 2) * part_rows] for j in range(groups)], axis=0
        )
        return jnp.where(parity == 1, high, low), jnp.where(parity == 1, low, high)

    def by_side(low, high):
        return jnp.where(side == 1, high, low), jnp.where(side == 1, low, high)

    def partial_products(c):
        for x in range(2):
            columns = pl.ds(pl.multiple_of((2 * x + c) * own, own), own)
            y = dot_tn(att_ref[:, columns], c_ref[...]).astype(BF16)
            gwb[0, c, x] = y[:, :half]
            gwb[1, c, x] = y[:, half:]

    def start_first():
        partial_products(1 - core)
        for copy in first_hop:
            copy.start()
        partial_products(core)

    def start_second():
        for i in (0, 1):
            first_hop[i].wait_recv()
            low, high = [gwb[i, core, x].astype(F32) + ra[i, x].astype(F32) for x in range(2)]
            if i == 0:
                keep, send = by_side(low, high)
            else:
                keep_low, send_low = by_parity(low)
                keep_high, send_high = by_parity(high)
                keep = jnp.concatenate([keep_low, keep_high], axis=0)
                send = jnp.concatenate([send_low, send_high], axis=0)
            k1[i] = keep
            s1[i] = send.astype(BF16)
            second_hop[i].start()

    def start_third():
        for i in (0, 1):
            second_hop[i].wait_recv()
            x = k1[i] + r1[i].astype(F32)
            keep, send = by_parity(x) if i == 0 else by_side(x[: own // 2], x[own // 2 :])
            k2[i] = keep
            s2[i] = send.astype(BF16)
            third_hop[i].start()

    def last_hop(o, slot, peer):
        return remote(sd.at[slot], rd.at[o], ring_send.at[o], ring_recv.at[o], 2 * peer + parity)

    def start_last():
        for i in (0, 1):
            third_hop[i].wait_recv()
            x = k2[i] + r2[i].astype(F32)
            k2[i] = x
            for j in range(groups):
                sd[j, i * part_rows : (i + 1) * part_rows] = x[
                    j * part_rows : (j + 1) * part_rows
                ].astype(BF16)
        for o in range(1, groups):
            peer = lax.rem(place + o, groups)
            last_hop(o, peer, peer).start()

    def finish_weight():
        mine = pl.ds(pl.multiple_of(place * part_rows, part_rows), part_rows)
        totals = [k2[i, mine] for i in (0, 1)]
        for o in range(1, groups):
            src = lax.rem(place + groups - o, groups)
            last_hop(o, src, src).wait_recv()
            x = rd[o].astype(F32)
            totals = [totals[0] + x[:part_rows], totals[1] + x[part_rows:]]
        gw_ref[:, :half] = totals[0]
        gw_ref[:, half:] = totals[1]
        for o in range(1, groups):
            peer = lax.rem(place + o, groups)
            last_hop(o, peer, peer).wait_send()
        for copy in first_hop + second_hop + third_hop:
            copy.wait_send()

    left = lax.rem(me + n - 1, n)
    right = lax.rem(me + 1, n)
    top = pl.ds(0, BLOCK)
    last = pl.ds(rows - BLOCK, BLOCK)
    bottom = pl.ds(rows + BLOCK, BLOCK)
    to_right = [
        remote(k_ref.at[last], kext.at[top], halo_send.at[0], halo_recv.at[0], right),
        remote(v_ref.at[last], vext.at[top], halo_send.at[1], halo_recv.at[1], right),
    ]
    to_left = [
        remote(k_ref.at[top], kext.at[bottom], halo_send.at[2], halo_recv.at[2], left),
        remote(v_ref.at[top], vext.at[bottom], halo_send.at[3], halo_recv.at[3], left),
    ]

    r_id, i_id = iota((SLOT, rows), 0), iota((SLOT, rows), 1)

    def pick(rid):
        base, hit = 0, jnp.zeros((SLOT, rows), jnp.bool_)
        for width in widths:
            count = rows // width
            inside = jnp.logical_and(rid >= base, rid < base + count)
            hit = jnp.logical_or(hit, jnp.logical_and(inside, i_id // width == rid - base))
            base += count
        return jnp.where(hit, 1.0, 0.0).astype(BF16)

    first1 = rows // widths[0]
    first2 = first1 + rows // widths[1]

    def row_scale(shape):
        rr = iota(shape, 0) % 8
        return jnp.where(
            rr < first1,
            1.0 / math.sqrt(widths[0]),
            jnp.where(rr < first2, 1.0 / math.sqrt(widths[1]), 1.0 / math.sqrt(widths[2])),
        )

    pooled = dot(pick(r_id), k_ref[...]) + dot(pick(r_id - 8), v_ref[...])
    pool[me] = (pooled * row_scale((SLOT, 1))).astype(BF16)

    for o in range(1, n):
        peer = lax.rem(me + o, n)
        remote(pool.at[me], pool.at[me], pool_send.at[o], pool_recv.at[o], peer).start()

    @pl.when(has_right)
    def _():
        for copy in to_right:
            copy.start()

    @pl.when(has_left)
    def _():
        for copy in to_left:
            copy.start()

    kext[BLOCK : BLOCK + rows] = k_ref[...]
    vext[BLOCK : BLOCK + rows] = v_ref[...]

    @pl.when(me == 0)
    def _():
        kext[0:BLOCK] = jnp.zeros((BLOCK, hidden), BF16)
        vext[0:BLOCK] = jnp.zeros((BLOCK, hidden), BF16)

    @pl.when(me == n - 1)
    def _():
        kext[rows + BLOCK :] = jnp.zeros((BLOCK, hidden), BF16)
        vext[rows + BLOCK :] = jnp.zeros((BLOCK, hidden), BF16)

    da_ref[...] = dot_nt(c_ref[...], w_ref[...]).astype(BF16)

    for b in range(halves):
        qb = (iota((256, 256), 0) % 128) // BLOCK + 1
        kb = iota((256, 256), 1) // BLOCK
        ok = jnp.abs(qb - kb) <= 1
        if b == 0:
            ok = jnp.logical_and(ok, jnp.logical_or(kb > 0, has_left))
        if b == halves - 1:
            ok = jnp.logical_and(ok, jnp.logical_or(kb < 3, has_right))
        bias[b] = jnp.where(ok, 0.0, MASKED)

    x_id, xi_id = iota((hr_rows, rows), 0) // heads, iota((hr_rows, rows), 1)
    head_mask = iota((hr_rows, hidden), 1) // HEAD_DIM == iota((hr_rows, hidden), 0) % heads
    for level, width in enumerate(widths):
        hit = xi_id // width == x_id * BLOCK // width
        rows_q = dot(jnp.where(hit, 1.0, 0.0).astype(BF16), q_ref[...]) * (1.0 / math.sqrt(width))
        rows_q = rows_q.astype(BF16).astype(F32) * scale
        qx[level] = jnp.where(head_mask, rows_q, 0.0).astype(BF16)

    cols = SLOT * n
    t_id = iota((hr_rows, cols), 0) // heads
    dev, rr = iota((hr_rows, cols), 1) // SLOT, iota((hr_rows, cols), 1) % SLOT
    same_one = dev // span_one == me // span_one
    same_two = dev // span_two == me // span_two
    gap = jnp.abs(me * first1 + t_id - dev * first1 - rr)
    allowed = (
        same_one & (rr < first1) & (gap > 1),
        same_two & jnp.logical_not(same_one) & (rr >= first1) & (rr < first2),
        jnp.logical_not(same_two) & (rr >= first2) & (rr < first2 + rows // widths[2]),
    )

    for o in range(1, n):
        src = lax.rem(me + n - o, n)
        remote(pool.at[src], pool.at[src], pool_send.at[o], pool_recv.at[o], src).wait_recv()
    coarse = pool[...].reshape(cols, hidden)
    s = jnp.full((hr_rows, cols), MASKED, F32)
    for level in range(3):
        s = jnp.where(allowed[level], dot_nt(qx[level], coarse), s)
    mc = jnp.max(s, axis=1, keepdims=True)
    ex = jnp.where(s > 0.5 * MASKED, jnp.exp(s - mc), 0.0)
    ec[...] = ex
    rolled = pltpu.roll(ex, 8, 1).astype(BF16)
    er[...] = rolled
    mcs[...] = jnp.broadcast_to(mc, (hr_rows, 128))
    lcs[...] = jnp.broadcast_to(jnp.sum(ex, axis=1, keepdims=True), (hr_rows, 128))

    def fold_heads(x):
        x = jnp.where(head_mask, x, 0.0)
        return [jnp.sum(x[t * heads : (t + 1) * heads], axis=0, keepdims=True) for t in range(blocks)]

    for t, row in enumerate(fold_heads(dot(rolled, coarse))):
        ncs[t : t + 1, :] = row

    @pl.when(has_left)
    def _():
        for copy in to_right:
            copy.wait_recv()

    @pl.when(has_right)
    def _():
        for copy in to_left:
            copy.wait_recv()

    low = iota((128, 128), 1) < HEAD_DIM

    def stack(x):
        zero = jnp.zeros_like(x)
        return jnp.concatenate([jnp.where(low, x, zero), jnp.where(low, zero, x)], axis=0)

    def choose(x):
        return jnp.where(low, x[:128], x[128:])

    def forward(p):
        lanes = pl.ds(pl.multiple_of(p * 128, 128), 128)
        for b in range(halves):
            u = p * halves + b
            mine, win = pl.ds(128 * b, 128), pl.ds(128 * b, 256)
            q2 = stack(q_ref[mine, lanes] * scale)
            s = dot_nt(q2, kext[win, lanes]) + bias[b]

            def per_row(ref):
                parts = []
                for h in range(2):
                    for t in (2 * b, 2 * b + 1):
                        row = ref[pl.ds(t * heads + 2 * p + h, 1), :]
                        parts.append(jnp.broadcast_to(row, (BLOCK, 128)))
                return jnp.concatenate(parts, axis=0)

            mcr = per_row(mcs)
            m = jnp.maximum(jnp.max(s, axis=1, keepdims=True), mcr)
            e = jnp.exp(s - jnp.concatenate([m, m], axis=1))
            f = jnp.exp(mcr - m)
            inv = 1.0 / (jnp.sum(e, axis=1, keepdims=True) + per_row(lcs) * f)
            nc = jnp.concatenate(
                [jnp.broadcast_to(ncs[2 * b + t : 2 * b + t + 1, lanes], (BLOCK, 128)) for t in (0, 1, 0, 1)],
                axis=0,
            )
            num = dot(e.astype(BF16), vext[win, lanes]) + nc * f
            att_ref[mine, lanes] = choose(num * inv).astype(BF16)
            e_ref[u] = e
            inv_ref[u] = inv
            wt_ref[u] = f * inv

    def in_twos(step, first, stop, together=2):
        def body(i, carry):
            for j in range(together):
                step(together * i + j)
            return carry

        lax.fori_loop(first // together, stop // together, body, 0)

    in_twos(forward, 0, pairs, 4)

    start_first()
    mixed_ref[...] = dot(att_ref[...], w_ref[...]).astype(BF16)

    def backward(p):
        lanes = pl.ds(pl.multiple_of(p * 128, 128), 128)
        carried = None
        for b in range(halves):
            u = p * halves + b
            mine, win = pl.ds(128 * b, 128), pl.ds(128 * b, 256)
            q2 = stack(q_ref[mine, lanes] * scale)
            d2 = stack(da_ref[mine, lanes])
            att = att_ref[mine, lanes].astype(F32)
            d2f = d2.astype(F32)
            prod = d2f * jnp.concatenate([att, att], axis=0)
            delta = jnp.sum(prod, axis=1, keepdims=True)
            inv = inv_ref[u]
            pr = e_ref[u] * jnp.concatenate([inv, inv], axis=1)
            kw = kext[win, lanes]
            ds = (pr * (dot_nt(d2, vext[win, lanes]) - delta)).astype(BF16)
            gqa[mine, lanes] = choose(dot(ds, kw)) * scale
            grads = [dot_tn(ds, q2), dot_tn(pr.astype(BF16), d2)]
            for i, acc in enumerate((dke, dve)):
                head = grads[i][:128] if b == 0 else grads[i][:128] + carried[i]
                acc[mine, lanes] = head
                if b == halves - 1:
                    acc[pl.ds(128 * (b + 1), 128), lanes] = grads[i][128:]
            carried = [x[128:] for x in grads]
            wt = wt_ref[u]
            for ref, x in ((g_ref, wt * d2f), (h_ref, wt * prod)):
                x = x[:128] + x[128:]
                for t in range(2):
                    ref[2 * b + t : 2 * b + t + 1, lanes] = jnp.sum(
                        x[t * BLOCK : (t + 1) * BLOCK], axis=0, keepdims=True
                    )

    in_twos(backward, 0, pairs // 4)
    start_second()
    in_twos(backward, pairs // 4, 3 * pairs // 4)
    start_third()
    in_twos(backward, 3 * pairs // 4, pairs)

    hs[0] = dke[rows + BLOCK :].astype(BF16)
    hs[1] = dve[rows + BLOCK :].astype(BF16)
    hs[2] = dke[0:BLOCK].astype(BF16)
    hs[3] = dve[0:BLOCK].astype(BF16)
    edge_right = [remote(hs.at[i], hr.at[i], edge_send.at[i], edge_recv.at[i], right) for i in (0, 1)]
    edge_left = [remote(hs.at[i], hr.at[i], edge_send.at[i], edge_recv.at[i], left) for i in (2, 3)]

    @pl.when(has_right)
    def _():
        for copy in edge_right:
            copy.start()

    @pl.when(has_left)
    def _():
        for copy in edge_left:
            copy.start()

    start_last()

    def spread(ref):
        x = jnp.concatenate(
            [jnp.broadcast_to(ref[t : t + 1, :], (heads, hidden)) for t in range(blocks)], axis=0
        )
        return jnp.where(head_mask, x, 0.0)

    gx = spread(g_ref).astype(BF16)
    hsum = jnp.sum(spread(h_ref), axis=1, keepdims=True)
    ds = ec[...] * (pltpu.roll(dot_nt(gx, coarse), cols - 8, 1) - hsum)
    grad = dot_tn(er[...], gx)
    mix = jnp.zeros((hr_rows, cols), F32)
    a_id, b_id = iota((hr_rows, hr_rows), 0), iota((hr_rows, hr_rows), 1)
    for level, width in enumerate(widths):
        dsl = jnp.where(allowed[level], ds, 0.0).astype(BF16)
        grad = grad + dot_tn(dsl, qx[level])
        span = width // BLOCK * heads
        same = (a_id // span == b_id // span) & (a_id % heads == b_id % heads)
        mix = mix + dot(jnp.where(same, 1.0, 0.0).astype(BF16), dsl) * (scale / math.sqrt(width))
    dcs[...] = grad.astype(BF16).reshape(n, SLOT, hidden)
    for o in range(1, n):
        peer = lax.rem(me + o, n)
        remote(dcs.at[peer], dcr.at[o], back_send.at[o], back_recv.at[o], peer).start()

    for t, row in enumerate(fold_heads(dot(mix.astype(BF16), coarse))):
        part = pl.ds(t * BLOCK, BLOCK)
        gq_ref[part, :] = (gqa[part, :] + row).astype(BF16)

    total = dcs[me].astype(F32)
    for o in range(1, n):
        src = lax.rem(me + n - o, n)
        remote(dcs.at[src], dcr.at[o], back_send.at[o], back_recv.at[o], src).wait_recv()
        total = total + dcr[o].astype(F32)
    total = total * row_scale((SLOT, 1))

    @pl.when(has_left)
    def _():
        for i, acc in ((0, dke), (1, dve)):
            edge_right[i].wait_recv()
            acc[BLOCK : 2 * BLOCK] += hr[i].astype(F32)

    @pl.when(has_right)
    def _():
        for i, acc in ((0, dke), (1, dve)):
            edge_left[i].wait_recv()
            acc[rows : rows + BLOCK] += hr[2 + i].astype(F32)

    for t in range(blocks):
        part = pl.ds(t * BLOCK, BLOCK)
        for base, acc, out in ((0, dke, gk_ref), (8, dve, gv_ref)):
            row = total[base + t : base + t + 1]
            second = base + first1 + t // 2
            third = base + first2 + t // 4
            row = row + total[second : second + 1] + total[third : third + 1]
            out[part, :] = (acc[pl.ds((t + 1) * BLOCK, BLOCK), :] + row).astype(BF16)

    finish_weight()
    for o in range(1, n):
        peer = lax.rem(me + o, n)
        remote(pool.at[me], pool.at[me], pool_send.at[o], pool_recv.at[o], peer).wait_send()
        remote(dcs.at[peer], dcr.at[o], back_send.at[o], back_recv.at[o], peer).wait_send()

    @pl.when(has_right)
    def _():
        for copy in to_right + edge_right:
            copy.wait_send()

    @pl.when(has_left)
    def _():
        for copy in to_left + edge_left:
            copy.wait_send()


def on_device(queries, keys, values, out_weight, cotangent):
    n = lax.axis_size("seq")
    rows, hidden = queries.shape[1:]
    span_one, span_two = max(2, n // 8), n // 2
    units = (hidden // 128) * (rows // 128)
    hrows = rows // BLOCK * HEADS
    ext = rows + 2 * BLOCK
    vm = pl.BlockSpec(memory_space=pltpu.VMEM)
    own, half = hidden // 4, hidden // 2
    act = jax.ShapeDtypeStruct((rows, hidden), BF16)
    dma = pltpu.SemaphoreType.DMA
    mixed, gw, gq, gk, gv = pl.pallas_call(
        functools.partial(kernel, n, span_one, span_two),
        out_shape=(act, jax.ShapeDtypeStruct((own // n, hidden), F32), act, act, act),
        in_specs=[vm] * 5,
        out_specs=(vm,) * 5,
        scratch_shapes=[
            pltpu.VMEM((ext, hidden), BF16),
            pltpu.VMEM((ext, hidden), BF16),
            pltpu.VMEM((n, SLOT, hidden), BF16),
            pltpu.VMEM((rows, hidden), BF16),
            pltpu.VMEM((rows, hidden), BF16),
            pltpu.VMEM((rows // 128, 256, 256), F32),
            pltpu.VMEM((3, hrows, hidden), BF16),
            pltpu.VMEM((hrows, SLOT * n), F32),
            pltpu.VMEM((hrows, SLOT * n), BF16),
            pltpu.VMEM((hrows, 128), F32),
            pltpu.VMEM((hrows, 128), F32),
            pltpu.VMEM((8, hidden), F32),
            pltpu.VMEM((units, 256, 256), F32),
            pltpu.VMEM((units, 256, 128), F32),
            pltpu.VMEM((units, 256, 128), F32),
            pltpu.VMEM((8, hidden), F32),
            pltpu.VMEM((8, hidden), F32),
            pltpu.VMEM((rows, hidden), F32),
            pltpu.VMEM((ext, hidden), F32),
            pltpu.VMEM((ext, hidden), F32),
            pltpu.VMEM((4, BLOCK, hidden), BF16),
            pltpu.VMEM((4, BLOCK, hidden), BF16),
            pltpu.VMEM((n, SLOT, hidden), BF16),
            pltpu.VMEM((n, SLOT, hidden), BF16),
            pltpu.VMEM((2, 2, 2, own, half), BF16),
            pltpu.VMEM((2, 2, own, half), BF16),
            pltpu.VMEM((2, own, half), BF16),
            pltpu.VMEM((2, own, half), BF16),
            pltpu.VMEM((2, own, half), F32),
            pltpu.VMEM((2, own // 2, half), BF16),
            pltpu.VMEM((2, own // 2, half), BF16),
            pltpu.VMEM((2, own // 2, half), F32),
            pltpu.VMEM((n // 2, 2 * own // n, half), BF16),
            pltpu.VMEM((n // 2, 2 * own // n, half), BF16),
            dma((n,)), dma((n,)), dma((4,)), dma((4,)), dma((n,)), dma((n,)), dma((4,)), dma((4,)),
            dma((6,)), dma((6,)), dma((n // 2,)), dma((n // 2,)),
        ],
        compiler_params=pltpu.CompilerParams(
            collective_id=0, has_side_effects=True, vmem_limit_bytes=56 * 1024 * 1024
        ),
    )(queries[0], keys[0], values[0], out_weight, cotangent[0])
    return mixed[None], gw, gq[None], gk[None], gv[None]


def solution(mesh):
    tokens = P("dp", "seq", None)
    return jax.shard_map(
        on_device,
        mesh=mesh,
        in_specs=(tokens, tokens, tokens, P(), tokens),
        out_specs=(tokens, P(("dp", "seq"), None), tokens, tokens, tokens),
        check_vma=False,
    )
```

```python
import functools
import math

import jax
import jax.numpy as jnp
from jax import lax
from jax.experimental import pallas as pl
from jax.experimental.pallas import tpu as pltpu
from jax.sharding import PartitionSpec as P

HEADS = 16
HEAD_DIM = 64
BLOCK = 64
MASKED = -1e30
SLOT = 16
F32 = jnp.float32
BF16 = jnp.bfloat16


def dot(a, b):
    return lax.dot_general(a, b, (((1,), (0,)), ((), ())), preferred_element_type=F32)


def dot_nt(a, b):
    return lax.dot_general(a, b, (((1,), (1,)), ((), ())), preferred_element_type=F32)


def dot_tn(a, b):
    return lax.dot_general(a, b, (((0,), (0,)), ((), ())), preferred_element_type=F32)


def iota(shape, dim):
    return lax.broadcasted_iota(jnp.int32, shape, dim)


def kernel(
    n, span_one, span_two,
    q_ref, k_ref, v_ref, w_ref, c_ref,
    mixed_ref, gw_ref, gq_ref, gk_ref, gv_ref,
    kext, vext, pool, da_ref, att_ref, bias, qx, ec, er, mcs, lcs, ncs, e_ref, inv_ref, wt_ref,
    g_ref, h_ref, gqa, dke, dve, hs, hr, dcs, dcr,
    gwb, ra, s1, r1, k1, s2, r2, k2, sd, rd,
    pool_send, pool_recv, halo_send, halo_recv, back_send, back_recv, edge_send, edge_recv,
    tree_send, tree_recv, ring_send, ring_recv,
):
    rows, hidden = q_ref.shape
    blocks = rows // BLOCK
    pairs = hidden // 128
    halves = rows // 128
    widths = (BLOCK, 2 * BLOCK, 4 * BLOCK)
    scale = 1.0 / math.sqrt(HEAD_DIM)
    me = lax.axis_index("seq")
    heads = HEADS
    hr_rows = blocks * heads
    has_left, has_right = me > 0, me < n - 1

    barrier = pltpu.get_barrier_semaphore()
    for o in range(1, n):
        pl.semaphore_signal(
            barrier, inc=1, device_id={"seq": lax.rem(me + o, n)}, device_id_type=pl.DeviceIdType.MESH
        )
    dp = lax.axis_index("dp")
    core, side = dp % 2, dp // 2
    mate, across = dp + 1 - 2 * core, lax.rem(dp + 2, 4)
    for peer in (mate, across):
        pl.semaphore_signal(
            barrier, inc=1, device_id={"dp": peer}, device_id_type=pl.DeviceIdType.MESH
        )
    pl.semaphore_wait(barrier, n + 1)

    def remote(src, dst, ssem, rsem, peer, axis="seq"):
        return pltpu.make_async_remote_copy(
            src_ref=src, dst_ref=dst, send_sem=ssem, recv_sem=rsem,
            device_id={axis: peer}, device_id_type=pl.DeviceIdType.MESH,
        )

    own = hidden // 4
    half = hidden // 2
    parity, place = me % 2, me // 2
    twin = me + 1 - 2 * parity
    groups = n // 2
    part_rows = own // n

    def tree(i, src, dst, axis):
        peer = {"core": mate, "x": across, "y": twin}[axis]
        return remote(src, dst, tree_send.at[i], tree_recv.at[i], peer, "seq" if axis == "y" else "dp")

    first_hop = [tree(i, gwb.at[i, 1 - core], ra.at[i], "core") for i in (0, 1)]
    second_hop = [tree(2 + i, s1.at[i], r1.at[i], "xy"[i]) for i in (0, 1)]
    third_hop = [tree(4 + i, s2.at[i], r2.at[i], "yx"[i]) for i in (0, 1)]

    def by_parity(x):
        low = jnp.concatenate(
            [x[2 * j * part_rows : (2 * j + 1) * part_rows] for j in range(groups)], axis=0
        )
        high = jnp.concatenate(
            [x[(2 * j + 1) * part_rows : (2 * j + 2) * part_rows] for j in range(groups)], axis=0
        )
        return jnp.where(parity == 1, high, low), jnp.where(parity == 1, low, high)

    def by_side(low, high):
        return jnp.where(side == 1, high, low), jnp.where(side == 1, low, high)

    def partial_products(c):
        for x in range(2):
            columns = pl.ds(pl.multiple_of((2 * x + c) * own, own), own)
            y = dot_tn(att_ref[:, columns], c_ref[...]).astype(BF16)
            gwb[0, c, x] = y[:, :half]
            gwb[1, c, x] = y[:, half:]

    def start_first():
        partial_products(1 - core)
        for copy in first_hop:
            copy.start()
        partial_products(core)

    def start_second():
        for i in (0, 1):
            first_hop[i].wait_recv()
            low, high = [gwb[i, core, x].astype(F32) + ra[i, x].astype(F32) for x in range(2)]
            if i == 0:
                keep, send = by_side(low, high)
            else:
                keep_low, send_low = by_parity(low)
                keep_high, send_high = by_parity(high)
                keep = jnp.concatenate([keep_low, keep_high], axis=0)
                send = jnp.concatenate([send_low, send_high], axis=0)
            k1[i] = keep
            s1[i] = send.astype(BF16)
            second_hop[i].start()

    def start_third():
        for i in (0, 1):
            second_hop[i].wait_recv()
            x = k1[i] + r1[i].astype(F32)
            keep, send = by_parity(x) if i == 0 else by_side(x[: own // 2], x[own // 2 :])
            k2[i] = keep
            s2[i] = send.astype(BF16)
            third_hop[i].start()

    def last_hop(o, slot, peer):
        return remote(sd.at[slot], rd.at[o], ring_send.at[o], ring_recv.at[o], 2 * peer + parity)

    def start_last():
        for i in (0, 1):
            third_hop[i].wait_recv()
            x = k2[i] + r2[i].astype(F32)
            k2[i] = x
            for j in range(groups):
                sd[j, i * part_rows : (i + 1) * part_rows] = x[
                    j * part_rows : (j + 1) * part_rows
                ].astype(BF16)
        for o in range(1, groups):
            peer = lax.rem(place + o, groups)
            last_hop(o, peer, peer).start()

    def finish_weight():
        mine = pl.ds(pl.multiple_of(place * part_rows, part_rows), part_rows)
        totals = [k2[i, mine] for i in (0, 1)]
        for o in range(1, groups):
            src = lax.rem(place + groups - o, groups)
            last_hop(o, src, src).wait_recv()
            x = rd[o].astype(F32)
            totals = [totals[0] + x[:part_rows], totals[1] + x[part_rows:]]
        gw_ref[:, :half] = totals[0]
        gw_ref[:, half:] = totals[1]
        for o in range(1, groups):
            peer = lax.rem(place + o, groups)
            last_hop(o, peer, peer).wait_send()
        for copy in first_hop + second_hop + third_hop:
            copy.wait_send()

    left = lax.rem(me + n - 1, n)
    right = lax.rem(me + 1, n)
    top = pl.ds(0, BLOCK)
    last = pl.ds(rows - BLOCK, BLOCK)
    bottom = pl.ds(rows + BLOCK, BLOCK)
    to_right = [
        remote(k_ref.at[last], kext.at[top], halo_send.at[0], halo_recv.at[0], right),
        remote(v_ref.at[last], vext.at[top], halo_send.at[1], halo_recv.at[1], right),
    ]
    to_left = [
        remote(k_ref.at[top], kext.at[bottom], halo_send.at[2], halo_recv.at[2], left),
        remote(v_ref.at[top], vext.at[bottom], halo_send.at[3], halo_recv.at[3], left),
    ]

    @pl.when(has_right)
    def _():
        for copy in to_right:
            copy.start()

    @pl.when(has_left)
    def _():
        for copy in to_left:
            copy.start()

    r_id, i_id = iota((SLOT, rows), 0), iota((SLOT, rows), 1)

    def pick(rid):
        base, hit = 0, jnp.zeros((SLOT, rows), jnp.bool_)
        for width in widths:
            count = rows // width
            inside = jnp.logical_and(rid >= base, rid < base + count)
            hit = jnp.logical_or(hit, jnp.logical_and(inside, i_id // width == rid - base))
            base += count
        return jnp.where(hit, 1.0, 0.0).astype(BF16)

    first1 = rows // widths[0]
    first2 = first1 + rows // widths[1]

    def row_scale(shape):
        rr = iota(shape, 0) % 8
        return jnp.where(
            rr < first1,
            1.0 / math.sqrt(widths[0]),
            jnp.where(rr < first2, 1.0 / math.sqrt(widths[1]), 1.0 / math.sqrt(widths[2])),
        )

    pooled = dot(pick(r_id), k_ref[...]) + dot(pick(r_id - 8), v_ref[...])
    pool[me] = (pooled * row_scale((SLOT, 1))).astype(BF16)

    for o in range(1, n):
        peer = lax.rem(me + o, n)
        remote(pool.at[me], pool.at[me], pool_send.at[o], pool_recv.at[o], peer).start()

    kext[BLOCK : BLOCK + rows] = k_ref[...]
    vext[BLOCK : BLOCK + rows] = v_ref[...]

    @pl.when(me == 0)
    def _():
        kext[0:BLOCK] = jnp.zeros((BLOCK, hidden), BF16)
        vext[0:BLOCK] = jnp.zeros((BLOCK, hidden), BF16)

    @pl.when(me == n - 1)
    def _():
        kext[rows + BLOCK :] = jnp.zeros((BLOCK, hidden), BF16)
        vext[rows + BLOCK :] = jnp.zeros((BLOCK, hidden), BF16)

    da_ref[...] = dot_nt(c_ref[...], w_ref[...]).astype(BF16)

    for b in range(halves):
        qb = (iota((256, 256), 0) % 128) // BLOCK + 1
        kb = iota((256, 256), 1) // BLOCK
        ok = jnp.abs(qb - kb) <= 1
        if b == 0:
            ok = jnp.logical_and(ok, jnp.logical_or(kb > 0, has_left))
        if b == halves - 1:
            ok = jnp.logical_and(ok, jnp.logical_or(kb < 3, has_right))
        bias[b] = jnp.where(ok, 0.0, MASKED)

    x_id, xi_id = iota((hr_rows, rows), 0) // heads, iota((hr_rows, rows), 1)
    head_mask = iota((hr_rows, hidden), 1) // HEAD_DIM == iota((hr_rows, hidden), 0) % heads
    for level, width in enumerate(widths):
        hit = xi_id // width == x_id * BLOCK // width
        rows_q = dot(jnp.where(hit, 1.0, 0.0).astype(BF16), q_ref[...]) * (1.0 / math.sqrt(width))
        rows_q = rows_q.astype(BF16).astype(F32) * scale
        qx[level] = jnp.where(head_mask, rows_q, 0.0).astype(BF16)

    cols = SLOT * n
    t_id = iota((hr_rows, cols), 0) // heads
    dev, rr = iota((hr_rows, cols), 1) // SLOT, iota((hr_rows, cols), 1) % SLOT
    same_one = dev // span_one == me // span_one
    same_two = dev // span_two == me // span_two
    gap = jnp.abs(me * first1 + t_id - dev * first1 - rr)
    allowed = (
        same_one & (rr < first1) & (gap > 1),
        same_two & jnp.logical_not(same_one) & (rr >= first1) & (rr < first2),
        jnp.logical_not(same_two) & (rr >= first2) & (rr < first2 + rows // widths[2]),
    )

    for o in range(1, n):
        src = lax.rem(me + n - o, n)
        remote(pool.at[src], pool.at[src], pool_send.at[o], pool_recv.at[o], src).wait_recv()
    coarse = pool[...].reshape(cols, hidden)
    s = jnp.full((hr_rows, cols), MASKED, F32)
    for level in range(3):
        s = jnp.where(allowed[level], dot_nt(qx[level], coarse), s)
    mc = jnp.max(s, axis=1, keepdims=True)
    ex = jnp.where(s > 0.5 * MASKED, jnp.exp(s - mc), 0.0)
    ec[...] = ex
    rolled = pltpu.roll(ex, 8, 1).astype(BF16)
    er[...] = rolled
    mcs[...] = jnp.broadcast_to(mc, (hr_rows, 128))
    lcs[...] = jnp.broadcast_to(jnp.sum(ex, axis=1, keepdims=True), (hr_rows, 128))

    def fold_heads(x):
        x = jnp.where(head_mask, x, 0.0)
        return [jnp.sum(x[t * heads : (t + 1) * heads], axis=0, keepdims=True) for t in range(blocks)]

    for t, row in enumerate(fold_heads(dot(rolled, coarse))):
        ncs[t : t + 1, :] = row

    @pl.when(has_left)
    def _():
        for copy in to_right:
            copy.wait_recv()

    @pl.when(has_right)
    def _():
        for copy in to_left:
            copy.wait_recv()

    low = iota((128, 128), 1) < HEAD_DIM

    def stack(x):
        zero = jnp.zeros_like(x)
        return jnp.concatenate([jnp.where(low, x, zero), jnp.where(low, zero, x)], axis=0)

    def choose(x):
        return jnp.where(low, x[:128], x[128:])

    def forward(p):
        lanes = pl.ds(pl.multiple_of(p * 128, 128), 128)
        for b in range(halves):
            u = p * halves + b
            mine, win = pl.ds(128 * b, 128), pl.ds(128 * b, 256)
            q2 = stack(q_ref[mine, lanes] * scale)
            s = dot_nt(q2, kext[win, lanes]) + bias[b]

            def per_row(ref):
                parts = []
                for h in range(2):
                    for t in (2 * b, 2 * b + 1):
                        row = ref[pl.ds(t * heads + 2 * p + h, 1), :]
                        parts.append(jnp.broadcast_to(row, (BLOCK, 128)))
                return jnp.concatenate(parts, axis=0)

            mcr = per_row(mcs)
            m = jnp.maximum(jnp.max(s, axis=1, keepdims=True), mcr)
            e = jnp.exp(s - jnp.concatenate([m, m], axis=1))
            f = jnp.exp(mcr - m)
            inv = 1.0 / (jnp.sum(e, axis=1, keepdims=True) + per_row(lcs) * f)
            nc = jnp.concatenate(
                [jnp.broadcast_to(ncs[2 * b + t : 2 * b + t + 1, lanes], (BLOCK, 128)) for t in (0, 1, 0, 1)],
                axis=0,
            )
            num = dot(e.astype(BF16), vext[win, lanes]) + nc * f
            att_ref[mine, lanes] = choose(num * inv).astype(BF16)
            e_ref[u] = e
            inv_ref[u] = inv
            wt_ref[u] = f * inv

    def in_twos(step, first, stop, together=2):
        def body(i, carry):
            for j in range(together):
                step(together * i + j)
            return carry

        lax.fori_loop(first // together, stop // together, body, 0)

    in_twos(forward, 0, pairs, 4)

    start_first()
    mixed_ref[...] = dot(att_ref[...], w_ref[...]).astype(BF16)

    def backward(p):
        lanes = pl.ds(pl.multiple_of(p * 128, 128), 128)
        carried = None
        for b in range(halves):
            u = p * halves + b
            mine, win = pl.ds(128 * b, 128), pl.ds(128 * b, 256)
            q2 = stack(q_ref[mine, lanes] * scale)
            d2 = stack(da_ref[mine, lanes])
            att = att_ref[mine, lanes].astype(F32)
            d2f = d2.astype(F32)
            prod = d2f * jnp.concatenate([att, att], axis=0)
            delta = jnp.sum(prod, axis=1, keepdims=True)
            inv = inv_ref[u]
            pr = e_ref[u] * jnp.concatenate([inv, inv], axis=1)
            kw = kext[win, lanes]
            ds = (pr * (dot_nt(d2, vext[win, lanes]) - delta)).astype(BF16)
            gqa[mine, lanes] = choose(dot(ds, kw)) * scale
            grads = [dot_tn(ds, q2), dot_tn(pr.astype(BF16), d2)]
            for i, acc in enumerate((dke, dve)):
                head = grads[i][:128] if b == 0 else grads[i][:128] + carried[i]
                acc[mine, lanes] = head
                if b == halves - 1:
                    acc[pl.ds(128 * (b + 1), 128), lanes] = grads[i][128:]
            carried = [x[128:] for x in grads]
            wt = wt_ref[u]
            for ref, x in ((g_ref, wt * d2f), (h_ref, wt * prod)):
                x = x[:128] + x[128:]
                for t in range(2):
                    ref[2 * b + t : 2 * b + t + 1, lanes] = jnp.sum(
                        x[t * BLOCK : (t + 1) * BLOCK], axis=0, keepdims=True
                    )

    in_twos(backward, 0, pairs // 4)
    start_second()
    in_twos(backward, pairs // 4, 3 * pairs // 4)
    start_third()
    in_twos(backward, 3 * pairs // 4, pairs)

    hs[0] = dke[rows + BLOCK :].astype(BF16)
    hs[1] = dve[rows + BLOCK :].astype(BF16)
    hs[2] = dke[0:BLOCK].astype(BF16)
    hs[3] = dve[0:BLOCK].astype(BF16)
    edge_right = [remote(hs.at[i], hr.at[i], edge_send.at[i], edge_recv.at[i], right) for i in (0, 1)]
    edge_left = [remote(hs.at[i], hr.at[i], edge_send.at[i], edge_recv.at[i], left) for i in (2, 3)]

    @pl.when(has_right)
    def _():
        for copy in edge_right:
            copy.start()

    @pl.when(has_left)
    def _():
        for copy in edge_left:
            copy.start()

    start_last()

    def spread(ref):
        x = jnp.concatenate(
            [jnp.broadcast_to(ref[t : t + 1, :], (heads, hidden)) for t in range(blocks)], axis=0
        )
        return jnp.where(head_mask, x, 0.0)

    gx = spread(g_ref).astype(BF16)
    hsum = jnp.sum(spread(h_ref), axis=1, keepdims=True)
    ds = ec[...] * (pltpu.roll(dot_nt(gx, coarse), cols - 8, 1) - hsum)
    grad = dot_tn(er[...], gx)
    mix = jnp.zeros((hr_rows, cols), F32)
    a_id, b_id = iota((hr_rows, hr_rows), 0), iota((hr_rows, hr_rows), 1)
    for level, width in enumerate(widths):
        dsl = jnp.where(allowed[level], ds, 0.0).astype(BF16)
        grad = grad + dot_tn(dsl, qx[level])
        span = width // BLOCK * heads
        same = (a_id // span == b_id // span) & (a_id % heads == b_id % heads)
        mix = mix + dot(jnp.where(same, 1.0, 0.0).astype(BF16), dsl) * (scale / math.sqrt(width))
    dcs[...] = grad.astype(BF16).reshape(n, SLOT, hidden)
    for o in range(1, n):
        peer = lax.rem(me + o, n)
        remote(dcs.at[peer], dcr.at[o], back_send.at[o], back_recv.at[o], peer).start()

    for t, row in enumerate(fold_heads(dot(mix.astype(BF16), coarse))):
        part = pl.ds(t * BLOCK, BLOCK)
        gq_ref[part, :] = (gqa[part, :] + row).astype(BF16)

    total = dcs[me].astype(F32)
    for o in range(1, n):
        src = lax.rem(me + n - o, n)
        remote(dcs.at[src], dcr.at[o], back_send.at[o], back_recv.at[o], src).wait_recv()
        total = total + dcr[o].astype(F32)
    total = total * row_scale((SLOT, 1))

    @pl.when(has_left)
    def _():
        for i, acc in ((0, dke), (1, dve)):
            edge_right[i].wait_recv()
            acc[BLOCK : 2 * BLOCK] += hr[i].astype(F32)

    @pl.when(has_right)
    def _():
        for i, acc in ((0, dke), (1, dve)):
            edge_left[i].wait_recv()
            acc[rows : rows + BLOCK] += hr[2 + i].astype(F32)

    for t in range(blocks):
        part = pl.ds(t * BLOCK, BLOCK)
        for base, acc, out in ((0, dke, gk_ref), (8, dve, gv_ref)):
            row = total[base + t : base + t + 1]
            second = base + first1 + t // 2
            third = base + first2 + t // 4
            row = row + total[second : second + 1] + total[third : third + 1]
            out[part, :] = (acc[pl.ds((t + 1) * BLOCK, BLOCK), :] + row).astype(BF16)

    finish_weight()
    for o in range(1, n):
        peer = lax.rem(me + o, n)
        remote(pool.at[me], pool.at[me], pool_send.at[o], pool_recv.at[o], peer).wait_send()
        remote(dcs.at[peer], dcr.at[o], back_send.at[o], back_recv.at[o], peer).wait_send()

    @pl.when(has_right)
    def _():
        for copy in to_right + edge_right:
            copy.wait_send()

    @pl.when(has_left)
    def _():
        for copy in to_left + edge_left:
            copy.wait_send()


def on_device(queries, keys, values, out_weight, cotangent):
    n = lax.axis_size("seq")
    rows, hidden = queries.shape[1:]
    span_one, span_two = max(2, n // 8), n // 2
    units = (hidden // 128) * (rows // 128)
    hrows = rows // BLOCK * HEADS
    ext = rows + 2 * BLOCK
    vm = pl.BlockSpec(memory_space=pltpu.VMEM)
    own, half = hidden // 4, hidden // 2
    act = jax.ShapeDtypeStruct((rows, hidden), BF16)
    dma = pltpu.SemaphoreType.DMA
    mixed, gw, gq, gk, gv = pl.pallas_call(
        functools.partial(kernel, n, span_one, span_two),
        out_shape=(act, jax.ShapeDtypeStruct((own // n, hidden), F32), act, act, act),
        in_specs=[vm] * 5,
        out_specs=(vm,) * 5,
        scratch_shapes=[
            pltpu.VMEM((ext, hidden), BF16),
            pltpu.VMEM((ext, hidden), BF16),
            pltpu.VMEM((n, SLOT, hidden), BF16),
            pltpu.VMEM((rows, hidden), BF16),
            pltpu.VMEM((rows, hidden), BF16),
            pltpu.VMEM((rows // 128, 256, 256), F32),
            pltpu.VMEM((3, hrows, hidden), BF16),
            pltpu.VMEM((hrows, SLOT * n), F32),
            pltpu.VMEM((hrows, SLOT * n), BF16),
            pltpu.VMEM((hrows, 128), F32),
            pltpu.VMEM((hrows, 128), F32),
            pltpu.VMEM((8, hidden), F32),
            pltpu.VMEM((units, 256, 256), F32),
            pltpu.VMEM((units, 256, 128), F32),
            pltpu.VMEM((units, 256, 128), F32),
            pltpu.VMEM((8, hidden), F32),
            pltpu.VMEM((8, hidden), F32),
            pltpu.VMEM((rows, hidden), F32),
            pltpu.VMEM((ext, hidden), F32),
            pltpu.VMEM((ext, hidden), F32),
            pltpu.VMEM((4, BLOCK, hidden), BF16),
            pltpu.VMEM((4, BLOCK, hidden), BF16),
            pltpu.VMEM((n, SLOT, hidden), BF16),
            pltpu.VMEM((n, SLOT, hidden), BF16),
            pltpu.VMEM((2, 2, 2, own, half), BF16),
            pltpu.VMEM((2, 2, own, half), BF16),
            pltpu.VMEM((2, own, half), BF16),
            pltpu.VMEM((2, own, half), BF16),
            pltpu.VMEM((2, own, half), F32),
            pltpu.VMEM((2, own // 2, half), BF16),
            pltpu.VMEM((2, own // 2, half), BF16),
            pltpu.VMEM((2, own // 2, half), F32),
            pltpu.VMEM((n // 2, 2 * own // n, half), BF16),
            pltpu.VMEM((n // 2, 2 * own // n, half), BF16),
            dma((n,)), dma((n,)), dma((4,)), dma((4,)), dma((n,)), dma((n,)), dma((4,)), dma((4,)),
            dma((6,)), dma((6,)), dma((n // 2,)), dma((n // 2,)),
        ],
        compiler_params=pltpu.CompilerParams(
            collective_id=0, has_side_effects=True, vmem_limit_bytes=56 * 1024 * 1024
        ),
    )(queries[0], keys[0], values[0], out_weight, cotangent[0])
    return mixed[None], gw, gq[None], gk[None], gv[None]


def solution(mesh):
    tokens = P("dp", "seq", None)
    return jax.shard_map(
        on_device,
        mesh=mesh,
        in_specs=(tokens, tokens, tokens, P(), tokens),
        out_specs=(tokens, P(("dp", "seq"), None), tokens, tokens, tokens),
        check_vma=False,
    )
```
